32 devices in a mesh: blk: 8 (over z, x), red: 4 (over y, core).
Axes of the slice: x: 2, y: 2, z: 4, core: 2. Of those that a mesh axis runs over, the one named last changes fastest.
Arguments:
- resid: float32 [1024, 16384], P('blk', 'red'), may hold values from -64 to 64
- norm_gain: float32 [16384], P('red'), may hold values from 0.1 to 1.9
- w_query: bfloat16 [16384, 16384], P('red', 'blk'), may hold values from -0.046875 to 0.046875
- w_key: bfloat16 [16384, 1024], P('red'), may hold values from -0.046875 to 0.046875
- w_value: bfloat16 [16384, 1024], P('red'), may hold values from -0.046875 to 0.046875
- w_out: bfloat16 [16384, 16384], P('blk', 'red'), may hold values from -0.046875 to 0.046875
- cache_key: bfloat16 [8192, 1024], P('red'), may hold values from -512 to 512
- cache_value: bfloat16 [8192, 1024], P('red'), may hold values from -8 to 8
- prefix_len: int32 [1], replicated, may hold values from 4096 to 8192
Outputs:
- updated: float32 [1024, 16384], P('blk', 'red')
The draws below stay inside these ranges and needn't reach their ends.
Inputs may be any that keep to these rules, and one draw needn't show every extreme that they name: `prefix_len`: cache slots below it hold the sequence's earlier tokens; the others are unused.
All inputs are finite; a program needn't handle non-finite values.
Results may differ from the reference program's by a relative error of at most 0.003.
The reference program's roundings to bfloat16 on the way count: a program that leaves them out, or rounds other values in their place, can miss the bound.
Values may be sent and summed in bfloat16 or wider, within the bound.
No kernel may reach another device: no remote copies, remote signals or barrier semaphores. Data moves between devices by JAX's collectives and lax.ppermute only.
A program may use at most 320 MiB of HBM per device.

```python
import math
import jax
import jax.numpy as jnp
from jax import lax

D = 16384
H = 128
KV = 8
HD = 128
SPAN = 1024
CACHE = 8192


def region_table(key, width):
    regions = jnp.arange(CACHE, dtype=jnp.int32) * 16 // CACHE
    table = jax.random.truncated_normal(key, -4.0, 4.0, (16, width), dtype=jnp.float32)
    return table[regions]


def draw_resid(key, part):
    key = jax.random.fold_in(key, 11)
    key_rows, key_cols, key_base = jax.random.split(key, 3)
    rows = jnp.exp(jax.random.uniform(key_rows, (SPAN, 1), jnp.float32, math.log(0.3), math.log(3.0)))
    cols = jnp.exp(jax.random.uniform(key_cols, (1, D), jnp.float32, math.log(0.5), math.log(2.0)))
    cols = cols * (1.0 + jnp.arange(D, dtype=jnp.float32)[None, :] / D)
    base = jax.random.truncated_normal(key_base, -4.0, 4.0, (SPAN, D), dtype=jnp.float32)
    return base * rows * cols


def draw_cache_key(key, part):
    key = jax.random.fold_in(key, 23)
    key_table, key_noise = jax.random.split(key, 2)
    width = KV * HD
    offsets = region_table(key_table, width)
    noise = jax.random.truncated_normal(key_noise, -4.0, 4.0, (CACHE, width), dtype=jnp.float32)
    keys = 0.7 * noise + 0.7 * offsets
    return keys.astype(jnp.bfloat16)


def draw_cache_value(key, part):
    key = jax.random.fold_in(key, 37)
    key_table, key_noise = jax.random.split(key, 2)
    width = KV * HD
    offsets = region_table(key_table, width)
    noise = jax.random.truncated_normal(key_noise, -4.0, 4.0, (CACHE, width), dtype=jnp.float32)
    return (0.6 * noise + offsets).astype(jnp.bfloat16)


def block_levels(rng, shape, cuts, low, top_value):
    level = 1.0
    for axis_at, parts in cuts:
        steps = jax.random.uniform(jax.random.fold_in(jax.random.fold_in(rng, 6), axis_at), (parts,), jnp.float32, low / len(cuts), top_value / len(cuts))
        level = level * jnp.repeat(jnp.exp(steps), shape[axis_at] // parts).reshape((-1,) + (1,) * (len(shape) - 1 - axis_at))
    return level


def centred(stream_key, dims, scale, limit, cuts=(), kind=jnp.bfloat16):
    drawn = jax.random.normal(stream_key, dims, jnp.float32) * scale
    if len(cuts) > 0:
        drawn = block_levels(stream_key, dims, cuts, -0.22, 0.18) * drawn
    return jnp.clip(drawn, min=-limit, max=limit).astype(kind)


def setup_inputs(seed: int = 0) -> dict:
    streams_of = jax.random.split(jax.random.key(seed), 10)
    resid = draw_resid(jax.random.fold_in(streams_of[9], 71), 0)
    norm_gain = jnp.clip(1.0 + 0.18 * jax.random.normal(streams_of[1], (D,), jnp.float32), 0.1, 1.9)
    w_query = centred(streams_of[2], (D, H * HD), D ** -0.5, 0.046875, ((0, 4), (1, 8)))
    w_key = centred(streams_of[3], (D, KV * HD), D ** -0.5, 0.046875, ((0, 4),))
    w_value = centred(streams_of[4], (D, KV * HD), D ** -0.5, 0.046875, ((0, 4),))
    w_out = centred(streams_of[5], (H * HD, D), (H * HD) ** -0.5, 0.046875, ((0, 8), (1, 4)))
    cache_key = draw_cache_key(jax.random.fold_in(streams_of[9], 71), 0)
    cache_value = draw_cache_value(jax.random.fold_in(streams_of[9], 71), 0)
    prefix_len = jax.random.randint(streams_of[8], (1,), CACHE // 2, CACHE + 1).astype(jnp.int32)
    return dict(resid=resid, norm_gain=norm_gain, w_query=w_query, w_key=w_key, w_value=w_value, w_out=w_out, cache_key=cache_key, cache_value=cache_value, prefix_len=prefix_len)


theta = 500000.0

def rotate(values, positions):
    half = values.shape[-1] // 2
    steps = jnp.arange(half, dtype=jnp.float32)
    freq = theta ** (-(steps * 2.0) / values.shape[-1])
    angle = positions.astype(jnp.float32)[:, None] * freq[None, :]
    cosine = jnp.cos(angle)[:, None, :]
    sine = jnp.sin(angle)[:, None, :]
    first = values[..., :half]
    second = values[..., half:]
    return jnp.concatenate([first * cosine - second * sine, second * cosine + first * sine], axis=-1)

def reference(resid, norm_gain, w_query, w_key, w_value, w_out, cache_key, cache_value, prefix_len):
    meansq = lax.optimization_barrier(jnp.mean(resid * resid, axis=1, keepdims=True))
    normed = (resid * lax.rsqrt(meansq + 1e-05) * norm_gain[None, :]).astype(jnp.bfloat16)
    query_raw = jnp.dot(normed, w_query, preferred_element_type=jnp.float32)
    key_raw = jnp.dot(normed, w_key, preferred_element_type=jnp.float32)
    value = jnp.dot(normed, w_value, preferred_element_type=jnp.float32).astype(jnp.bfloat16)
    start = prefix_len[0]
    positions = start + jnp.arange(SPAN, dtype=jnp.int32)
    query = rotate(query_raw.reshape(SPAN, H, HD), positions).astype(jnp.bfloat16)
    key = rotate(key_raw.reshape(SPAN, KV, HD), positions).astype(jnp.bfloat16)
    value = value.reshape(SPAN, KV, HD)
    old_keys = cache_key.reshape(CACHE, KV, HD)
    old_values = cache_value.reshape(CACHE, KV, HD)
    group = H // KV
    scale = HD ** (-0.5)
    cache_ok = (jnp.arange(CACHE, dtype=jnp.int32) < start)[None, None, :]
    every = jnp.arange(SPAN, dtype=jnp.int32)
    causal = (every[None, :] <= every[:, None])[:, None, :]

    def one_group(index):
        heads = lax.dynamic_slice_in_dim(query, index * group, group, 1).astype(jnp.float32)
        ok_keys = lax.dynamic_slice_in_dim(old_keys, index, 1, 1)[:, 0, :].astype(jnp.float32)
        ok_vals = lax.dynamic_slice_in_dim(old_values, index, 1, 1)[:, 0, :].astype(jnp.float32)
        new_keys = lax.dynamic_slice_in_dim(key, index, 1, 1)[:, 0, :].astype(jnp.float32)
        new_vals = lax.dynamic_slice_in_dim(value, index, 1, 1)[:, 0, :].astype(jnp.float32)
        old_scores = jnp.einsum('tgd,cd->tgc', heads, ok_keys) * scale
        new_scores = jnp.einsum('tgd,sd->tgs', heads, new_keys) * scale
        peak = jnp.maximum(lax.optimization_barrier(jnp.max(jnp.where(cache_ok, old_scores, -1e+30), axis=2)), lax.optimization_barrier(jnp.max(jnp.where(causal, new_scores, -1e+30), axis=2)))
        old_w = jnp.where(cache_ok, jnp.exp(old_scores - peak[:, :, None]), 0.0).astype(jnp.bfloat16).astype(jnp.float32)
        new_w = jnp.where(causal, jnp.exp(new_scores - peak[:, :, None]), 0.0).astype(jnp.bfloat16).astype(jnp.float32)
        total = lax.optimization_barrier(jnp.sum(old_w, axis=2)) + lax.optimization_barrier(jnp.sum(new_w, axis=2))
        mixed = jnp.einsum('tgc,cd->tgd', old_w, ok_vals) + jnp.einsum('tgs,sd->tgd', new_w, new_vals)
        return (mixed / total[:, :, None]).astype(jnp.bfloat16)
    blocks = lax.map(one_group, jnp.arange(KV, dtype=jnp.int32))
    attention = jnp.transpose(blocks, (1, 0, 2, 3)).reshape(SPAN, H * HD)
    return resid + jnp.dot(attention, w_out, preferred_element_type=jnp.float32)
```

```python
import functools
import math

import jax
import jax.numpy as jnp
from jax import lax
from jax.experimental import pallas as pl
from jax.experimental.pallas import tpu as pltpu
from jax.sharding import PartitionSpec as P

KV = 8
HD = 128
THETA = 500000.0
LOW = -1e30
RATE = HD**-0.5 / math.log(2.0)
SHRINK = 1.0 / 32.0
VMEM = 40 * 1024 * 1024


def tables(positions):
    half = HD // 2
    steps = jnp.arange(half, dtype=jnp.float32)
    freq = THETA ** (-(steps * 2.0) / HD)
    angle = positions.astype(jnp.float32)[..., None] * freq
    cosine, sine = jnp.cos(angle), jnp.sin(angle)
    return (
        jnp.concatenate([cosine, cosine], axis=-1),
        jnp.concatenate([-sine, sine], axis=-1),
    )


def fold(score, values, peak, acc):
    new_peak = jnp.maximum(peak, jnp.max(score, axis=1, keepdims=True))
    weights = jnp.exp2((score - new_peak) * RATE).astype(jnp.bfloat16)
    carry = jnp.exp2((peak - new_peak) * RATE)
    ones = jnp.ones(values.shape, values.dtype)
    term = jnp.dot(
        weights, jnp.concatenate([values, ones], axis=1), preferred_element_type=jnp.float32
    )
    return new_peak, acc * carry + term


def scores(query, keys):
    return lax.dot_general(
        query, keys, (((1,), (1,)), ((), ())), preferred_element_type=jnp.float32
    )


def cached_kernel(block, tile, start_ref, raw_ref, cos_ref, sin_ref, kv_ref, q_ref, peak_ref, acc_ref):
    start = start_ref[0]
    heads = raw_ref.shape[1] // HD
    cosine, sine = cos_ref[...], sin_ref[...]
    rotated = []
    for head in range(heads):
        at = slice(head * HD, (head + 1) * HD)
        raw = raw_ref[:, at]
        rotated.append(raw * cosine + pltpu.roll(raw, HD // 2, 1) * sine)
    q_ref[...] = jnp.concatenate(rotated, axis=0).astype(q_ref.dtype)
    peak_ref[...] = jnp.full(peak_ref.shape, LOW, jnp.float32)
    acc_ref[...] = jnp.zeros(acc_ref.shape, jnp.float32)

    def step(index, masked):
        here = pl.ds(pl.multiple_of(index * block, block), block)
        keys, values = kv_ref[here, :HD], kv_ref[here, HD:]
        for low in range(0, q_ref.shape[0], tile):
            rows = slice(low, low + tile)
            score = scores(q_ref[rows, :], keys)
            if masked:
                slot = index * block + lax.broadcasted_iota(jnp.int32, (1, block), 1)
                score = jnp.where(slot < start, score, LOW)
            peak, acc = fold(score, values, peak_ref[rows, :1], acc_ref[rows, :])
            peak_ref[rows, :] = jnp.broadcast_to(peak, (tile, HD))
            acc_ref[rows, :] = acc

    whole = start // block

    @pl.loop(0, whole)
    def _(index):
        step(index, False)

    @pl.when(start > whole * block)
    def _():
        step(whole, True)


def cached_part(start, raw, cosine, sine, cached):
    tokens, width = raw.shape
    rows = tokens * (width // HD)
    slots = cached.shape[0]
    block = min(1024, slots)
    tile = min(512, rows)
    vmem = pl.BlockSpec(memory_space=pltpu.VMEM)
    return pl.pallas_call(
        functools.partial(cached_kernel, block, tile),
        out_shape=(
            jax.ShapeDtypeStruct((rows, HD), jnp.bfloat16),
            jax.ShapeDtypeStruct((rows, HD), jnp.float32),
            jax.ShapeDtypeStruct((rows, 2 * HD), jnp.float32),
        ),
        in_specs=[pl.BlockSpec(memory_space=pltpu.SMEM)] + [vmem] * 4,
        out_specs=(vmem,) * 3,
        compiler_params=pltpu.CompilerParams(vmem_limit_bytes=VMEM),
        cost_estimate=pl.CostEstimate(
            flops=8 * rows * slots * HD,
            bytes_accessed=cached.size * 2 + raw.size * 8,
            transcendentals=rows * slots,
        ),
        name="cached_attention",
    )(start, raw, cosine, sine, cached)


def span_kernel(tile, q_ref, peak_ref, acc_ref, kv_ref, key_at_ref, query_at_ref, out_ref):
    tokens = out_ref.shape[0]
    keys, values = kv_ref[:, :HD], kv_ref[:, HD:]
    key_at = key_at_ref[...]
    for low in range(0, q_ref.shape[0], tile):
        rows = slice(low, low + tile)
        query_at = jnp.concatenate([query_at_ref[...]] * (tile // tokens), axis=0)[:, :1]
        score = jnp.where(key_at <= query_at, scores(q_ref[rows, :], keys), LOW)
        _, acc = fold(score, values, peak_ref[rows, :1], acc_ref[rows, :])
        mixed = (acc[:, :HD] / acc[:, HD:]).astype(out_ref.dtype)
        for part in range(tile // tokens):
            head = low // tokens + part
            out_ref[:, head * HD : (head + 1) * HD] = mixed[part * tokens : (part + 1) * tokens]


def span_part(query, peak, acc, fresh, key_at, query_at):
    tokens = query_at.shape[0]
    rows = query.shape[0]
    vmem = pl.BlockSpec(memory_space=pltpu.VMEM)
    return pl.pallas_call(
        functools.partial(span_kernel, min(512, rows)),
        out_shape=jax.ShapeDtypeStruct((tokens, rows // tokens * HD), jnp.bfloat16),
        in_specs=[vmem] * 6,
        out_specs=vmem,
        compiler_params=pltpu.CompilerParams(vmem_limit_bytes=VMEM),
        cost_estimate=pl.CostEstimate(
            flops=8 * rows * fresh.shape[0] * HD,
            bytes_accessed=rows * HD * 16,
            transcendentals=rows * fresh.shape[0],
        ),
        name="span_attention",
    )(query, peak, acc, fresh, key_at, query_at)


def on_device(resid, norm_gain, w_query, w_key, w_value, w_out, cache_key, cache_value, prefix_len):
    blk_count, red_count = lax.axis_size("blk"), lax.axis_size("red")
    blk_at, red_at = lax.axis_index("blk"), lax.axis_index("red")
    start = prefix_len[0]
    mine, width = resid.shape
    far_count = blk_count // 2
    far_at, near_at = blk_at // 2, blk_at % 2
    bits = [1 << k for k in range(red_count.bit_length() - 1)]

    def swap_red(value, bit):
        return lax.ppermute(value, "red", [(k, k ^ bit) for k in range(red_count)])

    def swap_near(value):
        return lax.ppermute(value, "blk", [(k, k ^ 1) for k in range(blk_count)])

    def move_far(value, pairs):
        pairs = [(2 * a + k, 2 * b + k) for a, b in pairs for k in range(2)]
        return lax.ppermute(value, "blk", pairs)

    line = far_count == 4
    if line:
        at_end = (far_at == 0) | (far_at == 3)
        pairs_out = [(1, 0), (2, 3)]
        pairs_in = [(0, 1), (3, 2)]
        middle = [(1, 2), (2, 1)]
        owners = [
            far_at,
            far_at ^ 1,
            far_at ^ jnp.where(at_end, 2, 3),
            far_at ^ jnp.where(at_end, 3, 2),
        ]
    else:
        owners = [(far_at + j) % far_count for j in range(far_count)]

    def spread(own):
        if line:
            a1 = move_far(own, pairs_out + pairs_in)
            b1 = move_far(own, middle)
            a2 = move_far(b1, pairs_out)
            b2 = move_far(a1, middle)
            a3 = move_far(b2, pairs_out)
            return [own, a1, jnp.where(at_end, a2, b1), jnp.where(at_end, a3, b2)]
        ring = range(far_count)
        return [own] + [
            move_far(own, [((k + j) % far_count, k) for k in ring]) for j in ring if j > 0
        ]

    def collect(parts):
        small = lambda value: value.astype(jnp.float16)
        wide = lambda value: value.astype(jnp.float32)
        if line:
            own, s1, s2, s3 = parts
            a3 = move_far(small(s3), pairs_in)
            a2 = move_far(small(s2), pairs_in)
            b2 = move_far(small(s3 + wide(a3)), middle)
            b1 = move_far(small(s2 + wide(a2)), middle)
            a1 = move_far(small(s1 + wide(b2)), pairs_out + pairs_in)
            return own + wide(a1) + wide(b1)
        total = parts[0]
        ring = range(far_count)
        for j in ring:
            if j > 0:
                moved = move_far(small(parts[j]), [(k, (k + j) % far_count) for k in ring])
                total = total + wide(moved)
        return total

    rows = 2 * mine
    here = rows // red_count
    low = 0
    for k, bit in enumerate(bits):
        low = low + ((red_at // bit) % 2) * (rows >> (k + 1))
    in_block = jnp.arange(mine, dtype=jnp.int32)
    token_at = [
        jnp.concatenate([(owner * 2 + (near_at ^ k)) * mine + in_block for k in range(2)])
        for owner in owners
    ]
    query_at = [lax.dynamic_slice_in_dim(at, low, here) for at in token_at]
    turns = [tables(start + at) for at in query_at]

    def sum_red(value):
        for bit in bits:
            half = value.shape[0] // 2
            side = (red_at // bit) % 2
            keep = lax.dynamic_slice_in_dim(value, side * half, half)
            send = lax.dynamic_slice_in_dim(value, (1 - side) * half, half)
            value = keep + swap_red(send, bit)
        return value

    def join_red(value):
        for bit in reversed(bits):
            got = swap_red(value, bit)
            upper = (red_at // bit) % 2 == 1
            value = jnp.where(
                upper, jnp.concatenate([got, value]), jnp.concatenate([value, got])
            )
        return value

    head_at = blk_at // (blk_count // KV)
    one_head = lambda value: lax.dynamic_slice_in_dim(value, head_at * HD, HD, 1)
    cached = lax.all_gather(
        jnp.concatenate([one_head(cache_key), one_head(cache_value)], axis=1),
        "red",
        axis=0,
        tiled=True,
    )
    w_fresh = jnp.concatenate([one_head(w_key), one_head(w_value)], axis=1)

    total_sq = jnp.sum(resid * resid, axis=1)
    for bit in bits:
        total_sq = total_sq + swap_red(total_sq, bit)
    normed = (
        resid * lax.rsqrt(total_sq[:, None] / (width * red_count) + 1e-05) * norm_gain[None, :]
    ).astype(jnp.bfloat16)

    arrived = [jnp.concatenate([part, swap_near(part)]) for part in spread(normed)]

    def fresh_part(slots):
        raw = [
            jnp.dot(arrived[j], w_fresh, preferred_element_type=jnp.float32) for j in slots
        ]
        summed = sum_red(jnp.concatenate(raw, axis=1)).reshape(here, len(slots), 2, HD)
        key_raw, value = summed[:, :, 0], summed[:, :, 1]
        cosine = jnp.stack([turns[j][0] for j in slots], axis=1)
        sine = jnp.stack([turns[j][1] for j in slots], axis=1)
        key = key_raw * cosine + jnp.roll(key_raw, HD // 2, axis=-1) * sine
        both = jnp.stack([key, value], axis=2).astype(jnp.bfloat16)
        both = join_red(both.reshape(here, len(slots) * 2 * HD))
        return [both[:, k * 2 * HD : (k + 1) * 2 * HD] for k in range(len(slots))]

    slots = range(far_count)
    fresh = fresh_part(slots[:-1]) + fresh_part(slots[-1:])
    fresh = jnp.concatenate(fresh)
    key_at = jnp.concatenate(token_at)[None, :]

    old = []
    for j in slots:
        raw = sum_red(jnp.dot(arrived[j], w_query, preferred_element_type=jnp.float32))
        old.append(cached_part(prefix_len, raw, turns[j][0], turns[j][1], cached))

    parts = [None] * far_count
    for j in reversed(slots):
        at = jnp.broadcast_to(query_at[j][:, None], (here, HD))
        attention = join_red(span_part(*old[j], fresh, key_at, at))
        out = jnp.dot(attention, w_out, preferred_element_type=jnp.float32) * SHRINK
        out = out.astype(jnp.float16)
        got = swap_near(out[mine:])
        parts[j] = out[:mine].astype(jnp.float32) + got.astype(jnp.float32)
    return resid + collect(parts) * (1.0 / SHRINK)


def solution(mesh):
    placed = (
        P("blk", "red"),
        P("red"),
        P("red", "blk"),
        P("red", None),
        P("red", None),
        P("blk", "red"),
        P("red", None),
        P("red", None),
        P(),
    )
    return jax.shard_map(
        on_device, mesh=mesh, in_specs=placed, out_specs=P("blk", "red"), check_vma=False
    )
```

```python
import functools
import math

import jax
import jax.numpy as jnp
from jax import lax
from jax.experimental import pallas as pl
from jax.experimental.pallas import tpu as pltpu
from jax.sharding import PartitionSpec as P

KV = 8
HD = 128
THETA = 500000.0
LOW = -1e30
RATE = HD**-0.5 / math.log(2.0)
SHRINK = 1.0 / 32.0
MIB = 1024 * 1024
PIECES = 2
COST = pl.CostEstimate(flops=0, bytes_accessed=0, transcendentals=0)


def tables(positions):
    half = HD // 2
    steps = jnp.arange(half, dtype=jnp.float32)
    freq = THETA ** (-(steps * 2.0) / HD)
    angle = positions.astype(jnp.float32)[..., None] * freq
    cosine, sine = jnp.cos(angle), jnp.sin(angle)
    return (
        jnp.concatenate([cosine, cosine], axis=-1),
        jnp.concatenate([-sine, sine], axis=-1),
    )


def fold(parts, peak, acc):
    lanes = [score[:, at : at + HD] for score, _ in parts for at in range(0, score.shape[1], HD)]
    top = jnp.max(functools.reduce(jnp.maximum, lanes), axis=1, keepdims=True)
    new_peak = jnp.maximum(peak, top)
    carry = jnp.exp2((peak - new_peak) * RATE)
    acc = acc * jnp.concatenate([carry, carry], axis=1)
    for score, values in parts:
        shift = jnp.concatenate([new_peak] * (score.shape[1] // HD), axis=1)
        weights = jnp.exp2((score - shift) * RATE).astype(jnp.bfloat16)
        both = jnp.concatenate([values, jnp.ones(values.shape, values.dtype)], axis=1)
        acc = acc + jnp.dot(weights, both, preferred_element_type=jnp.float32)
    return new_peak, acc


def scores(query, keys):
    return lax.dot_general(
        query, keys, (((1,), (1,)), ((), ())), preferred_element_type=jnp.float32
    )


def attention_kernel(base_at, far_count, slot, unit, tile, cached, spanned, *refs):
    refs = list(refs)
    facts_ref = refs.pop(0)
    if cached:
        keep_ref, got_ref, cos_ref, sin_ref, key_ref, value_ref = refs[:6]
        refs = refs[6:]
    else:
        old_q_ref, old_peak_ref, old_acc_ref = refs[:3]
        refs = refs[3:]
    if spanned:
        fresh_ref, out_ref = refs[:2]
        refs = refs[2:]
    q_ref, peak_ref, acc_ref = refs if cached else (old_q_ref, old_peak_ref, old_acc_ref)
    start = facts_ref[0]
    rows_here = q_ref.shape[0]
    tiles = [slice(low, low + tile) for low in range(0, rows_here, tile)]

    def step(base, count, masked):
        for rows in tiles:
            parts = []
            for k in range(count):
                low = pl.multiple_of(base + k * unit, unit)
                here = pl.ds(low, unit)
                score = jnp.dot(
                    q_ref[rows, :], key_ref[:, here], preferred_element_type=jnp.float32
                )
                if masked and k == count - 1:
                    at = low + lax.broadcasted_iota(jnp.int32, (1, unit), 1)
                    score = jnp.where(at < start, score, LOW)
                parts.append((score, value_ref[here, :]))
            peak_ref[rows, :], acc_ref[rows, :] = fold(parts, peak_ref[rows, :], acc_ref[rows, :])

    if cached:
        tokens = keep_ref.shape[0]
        mine = slice(slot * tokens, (slot + 1) * tokens)
        cosine, sine = cos_ref[mine, :], sin_ref[mine, :]
        rotated = []
        for head in range(keep_ref.shape[1] // HD):
            at = slice(head * HD, (head + 1) * HD)
            raw = keep_ref[:, at] + got_ref[:, at]
            rotated.append(raw * cosine + pltpu.roll(raw, HD // 2, 1) * sine)
        q_ref[...] = jnp.concatenate(rotated, axis=0).astype(q_ref.dtype)
        peak_ref[...] = jnp.full(peak_ref.shape, LOW, jnp.float32)
        acc_ref[...] = jnp.zeros(acc_ref.shape, jnp.float32)
        pairs = start // (2 * unit)
        done = pairs * (2 * unit)

        @pl.loop(0, pairs)
        def _(index):
            step(index * (2 * unit), 2, False)

        @pl.when((start > done) & (start <= done + unit))
        def _():
            step(done, 1, True)

        @pl.when(start > done + unit)
        def _():
            step(done, 2, True)

    if spanned:
        tokens = out_ref.shape[0]
        keys, values = fresh_ref[:, :HD], fresh_ref[:, HD:]
        far, near = facts_ref[base_at - 2], facts_ref[base_at - 1]
        own = fresh_ref.shape[0] // (2 * far_count)
        in_block = lax.broadcasted_iota(jnp.int32, (1, own), 1)
        key_at = jnp.concatenate(
            [
                in_block + ((far ^ d) * 2 + (near ^ k)) * own
                for d in range(far_count)
                for k in range(2)
            ],
            axis=1,
        )
        query_at = facts_ref[base_at + slot] + lax.broadcasted_iota(jnp.int32, (tokens, 1), 0)
        query_at = jnp.concatenate([query_at] * (tile // tokens), axis=0)
        for rows in tiles:
            score = jnp.where(key_at <= query_at, scores(q_ref[rows, :], keys), LOW)
            _, acc = fold([(score, values)], peak_ref[rows, :], acc_ref[rows, :])
            mixed = (acc[:, :HD] / acc[:, HD:]).astype(out_ref.dtype)
            for part in range(tile // tokens):
                head = rows.start // tokens + part
                out_ref[:, head * HD : (head + 1) * HD] = mixed[
                    part * tokens : (part + 1) * tokens
                ]


def attend(base_at, far_count, slot, facts, tokens, rows, old, new):
    cached = len(old) == 6
    spanned = new is not None
    unit = min(1024, old[5].shape[0] // 2) if cached else 0
    tile = min(256, rows)
    vmem = pl.BlockSpec(memory_space=pltpu.VMEM)
    state = [
        ((rows, HD), jnp.bfloat16),
        ((rows, HD), jnp.float32),
        ((rows, 2 * HD), jnp.float32),
    ]
    if spanned:
        out_shape = jax.ShapeDtypeStruct((tokens, rows // tokens * HD), jnp.bfloat16)
    else:
        out_shape = tuple(jax.ShapeDtypeStruct(*one) for one in state)
    operands = [*old, *([new] if spanned else [])]
    return pl.pallas_call(
        functools.partial(attention_kernel, base_at, far_count, slot, unit, tile, cached, spanned),
        out_shape=out_shape,
        in_specs=[pl.BlockSpec(memory_space=pltpu.SMEM)] + [vmem] * len(operands),
        out_specs=vmem if spanned else (vmem,) * 3,
        scratch_shapes=[pltpu.VMEM(*one) for one in state] if cached and spanned else [],
        compiler_params=pltpu.CompilerParams(vmem_limit_bytes=(9 if cached else 5) * MIB),
        cost_estimate=pl.CostEstimate(
            flops=8 * rows * HD * (old[5].shape[0] + new.shape[0]) if cached and spanned else 0,
            bytes_accessed=0,
            transcendentals=0,
        ),
        name="attention",
    )(facts, *operands)


def small_call(kernel, name, out_shape, facts, *operands):
    vmem = pl.BlockSpec(memory_space=pltpu.VMEM)
    return pl.pallas_call(
        kernel,
        out_shape=out_shape,
        in_specs=[pl.BlockSpec(memory_space=pltpu.SMEM)] + [vmem] * len(operands),
        out_specs=jax.tree.map(lambda _: vmem, out_shape),
        compiler_params=pltpu.CompilerParams(vmem_limit_bytes=4 * MIB),
        cost_estimate=COST,
        name=name,
    )(facts, *operands)


def cut_kernel(fact, facts_ref, keep_ref, got_ref, mine_ref, send_ref):
    half = mine_ref.shape[0]
    upper = facts_ref[fact] == 1
    low, high = (keep_ref[at, :] + got_ref[at, :] for at in (slice(0, half), slice(half, None)))
    mine_ref[...] = jnp.where(upper, high, low)
    send_ref[...] = jnp.where(upper, low, high)


def cut(fact, facts, keep, got):
    out = jax.ShapeDtypeStruct((keep.shape[0] // 2, keep.shape[1]), keep.dtype)
    return small_call(functools.partial(cut_kernel, fact), "cut", (out, out), facts, keep, got)


def join_kernel(fact, facts_ref, own_ref, got_ref, out_ref):
    half = own_ref.shape[1]
    upper = facts_ref[fact] == 1

    @pl.when(upper)
    def _():
        out_ref[:, :half] = got_ref[...]
        out_ref[:, half:] = own_ref[...]

    @pl.when(jnp.logical_not(upper))
    def _():
        out_ref[:, :half] = own_ref[...]
        out_ref[:, half:] = got_ref[...]


def join(fact, facts, own, got):
    count, half, width = own.shape
    if half % 16:
        upper = facts[fact] == 1
        return jnp.where(
            upper, jnp.concatenate([got, own], axis=1), jnp.concatenate([own, got], axis=1)
        )
    out = jax.ShapeDtypeStruct((count, 2 * half, width), own.dtype)
    return small_call(functools.partial(join_kernel, fact), "join", out, facts, own, got)


def merge_kernel(facts_ref, own_ref, got_ref, key_ref, value_ref):
    count, rows, _ = own_ref.shape
    for side in range(2):

        @pl.when(facts_ref[2] == side)
        def _():
            for k in range(count):
                for at, ref in ((2 * k + side, own_ref), (2 * k + 1 - side, got_ref)):
                    here = slice(at * rows, (at + 1) * rows)
                    key_ref[:, here] = ref[k, :, :HD].astype(jnp.float32).T.astype(key_ref.dtype)
                    value_ref[here, :] = ref[k, :, HD:]


def merge(facts, own, got):
    slots = 2 * own.shape[0] * own.shape[1]
    out = (
        jax.ShapeDtypeStruct((HD, slots), own.dtype),
        jax.ShapeDtypeStruct((slots, HD), own.dtype),
    )
    return small_call(merge_kernel, "merge", out, facts, own, got)


def pick_kernel(facts_ref, a_ref, b_ref, out_ref):
    @pl.when(facts_ref[1] == 1)
    def _():
        out_ref[...] = a_ref[...]

    @pl.when(facts_ref[1] != 1)
    def _():
        out_ref[...] = b_ref[...]


def pick(facts, a, b):
    return small_call(pick_kernel, "pick", jax.ShapeDtypeStruct(a.shape, a.dtype), facts, a, b)


def halves_kernel(blocks, tile, facts_ref, *refs):
    lhs, refs = refs[:blocks], refs[blocks:]
    w_refs, (keep_ref, send_ref) = refs[:-2], refs[-2:]
    rows, per_half = lhs[0].shape[0], blocks // 2
    upper, place = facts_ref[2] == 1, facts_ref[2] * 0
    for k in range(per_half.bit_length() - 1):
        place = place + facts_ref[3 + k] * (per_half >> (k + 1))
    both = jnp.concatenate([ref[...] for ref in lhs], axis=0)
    low = 0
    for w_ref in w_refs:

        @pl.loop(0, w_ref.shape[1] // tile)
        def _(step, low=low, w_ref=w_ref):
            at = pl.multiple_of(step * tile, tile)
            out = jnp.dot(both, w_ref[:, pl.ds(at, tile)], preferred_element_type=jnp.float32)
            here = pl.ds(pl.multiple_of(low + at, tile), tile)
            half = per_half * rows
            first = jnp.where(upper, out[half:], out[:half])
            second = jnp.where(upper, out[:half], out[half:])
            for k in range(per_half):
                to = pl.ds(pl.multiple_of((place ^ k) * rows, rows), rows)
                keep_ref[to, here] = first[k * rows : (k + 1) * rows]
                send_ref[to, here] = second[k * rows : (k + 1) * rows]

        low += w_ref.shape[1]


def halves(facts, lhs, weights):
    rows = lhs[0].shape[0] * len(lhs) // 2
    width = sum(w.shape[1] for w in weights)
    out = jax.ShapeDtypeStruct((rows, width), jnp.float32)
    vmem = pl.BlockSpec(memory_space=pltpu.VMEM)
    operands = [*lhs, *weights]
    return pl.pallas_call(
        functools.partial(halves_kernel, len(lhs), min(512, weights[0].shape[1])),
        out_shape=(out, out),
        in_specs=[pl.BlockSpec(memory_space=pltpu.SMEM)] + [vmem] * len(operands),
        out_specs=(vmem, vmem),
        compiler_params=pltpu.CompilerParams(vmem_limit_bytes=5 * MIB),
        cost_estimate=pl.CostEstimate(
            flops=4 * rows * weights[0].shape[0] * width, bytes_accessed=0, transcendentals=0
        ),
        name="halves",
    )(facts, *operands)


def pack_kernel(low, shift, where_at, facts_ref, keep_ref, got_ref, cos_ref, sin_ref, same_ref, other_ref):
    few = keep_ref.shape[0]
    cosine, sine = cos_ref[low : low + few, :], sin_ref[low : low + few, :]
    far, near = facts_ref[where_at], facts_ref[where_at + 1]
    for d in range(same_ref.shape[0]):
        for k, out_ref in enumerate((same_ref, other_ref)):
            head = ((far ^ d) * 2 + (near ^ k)) >> shift
            raw, value = (
                keep_ref[:, pl.ds(pl.multiple_of(at * HD, HD), HD)]
                + got_ref[:, pl.ds(pl.multiple_of(at * HD, HD), HD)]
                for at in (head, KV + head)
            )
            both = [raw * cosine + pltpu.roll(raw, HD // 2, 1) * sine, value]
            out_ref[d] = jnp.concatenate(both, axis=1).astype(out_ref.dtype)


def pack(low, shift, where_at, count, facts, keep, got, cosine, sine):
    out = jax.ShapeDtypeStruct((count, keep.shape[0], 2 * HD), jnp.bfloat16)
    kernel = functools.partial(pack_kernel, low, shift, where_at)
    return small_call(kernel, "pack", (out, out), facts, keep, got, cosine, sine)


def on_device(resid, norm_gain, w_query, w_key, w_value, w_out, cache_key, cache_value, prefix_len):
    blk_count, red_count = lax.axis_size("blk"), lax.axis_size("red")
    blk_at, red_at = lax.axis_index("blk"), lax.axis_index("red")
    start = prefix_len[0]
    mine, width = resid.shape
    far_count = blk_count // 2
    far_at, near_at = blk_at // 2, blk_at % 2
    bits = [1 << k for k in range(red_count.bit_length() - 1)]

    def swap_red(value, bit):
        return lax.ppermute(value, "red", [(k, k ^ bit) for k in range(red_count)])

    def swap_near(value):
        return lax.ppermute(value, "blk", [(k, k ^ 1) for k in range(blk_count)])

    def move_far(value, pairs):
        pairs = [(2 * a + k, 2 * b + k) for a, b in pairs for k in range(2)]
        return lax.ppermute(value, "blk", pairs)

    line = far_count == 4
    if line:
        at_end = (far_at == 0) | (far_at == 3)
        pairs_out = [(1, 0), (2, 3)]
        pairs_in = [(0, 1), (3, 2)]
        middle = [(1, 2), (2, 1)]
        owners = [
            far_at,
            far_at ^ 1,
            far_at ^ jnp.where(at_end, 2, 3),
            far_at ^ jnp.where(at_end, 3, 2),
        ]
    else:
        owners = [(far_at + j) % far_count for j in range(far_count)]

    def spread(own):
        if not line:
            ring = range(far_count)
            return [move_far(own, [((k + j) % far_count, k) for k in ring]) for j in ring if j > 0]
        a1 = move_far(own, pairs_out + pairs_in)
        b1 = move_far(own, middle)
        return [a1, b1, move_far(b1, pairs_out), move_far(a1, middle)]

    def arrive(hops, facts, *others):
        if not line:
            return hops
        a1, b1, a2, b2 = hops
        a3 = move_far(after(b2, *others), pairs_out)
        return [a1, pick(facts, a2, b1), pick(facts, a3, b2)]

    wide = lambda value: value.astype(jnp.float32)

    def add(terms, *others):
        return sum(map(wide, [*terms[:-1], after(terms[-1], *others)])).astype(jnp.float16)

    def collect(parts, first):
        own = [list(terms) for terms in parts[0]]
        if line:
            a1 = [move_far(value, pairs_out + pairs_in) for value in first]
            s2, s3 = parts[2:]
            last = first[-1]
            stages = {}

            def go(name, terms, pairs):
                nonlocal last
                last = add(terms, last)
                stages[name] = move_far(last, pairs)

            go("a3", s3[0], pairs_in)
            go("a3+", s3[1], pairs_in)
            go("b2", s3[0] + [stages["a3"]], middle)
            go("a2", s2[0], pairs_in)
            go("b2+", s3[1] + [stages["a3+"]], middle)
            go("c1", [stages["b2"]], pairs_out)
            go("a2+", s2[1], pairs_in)
            go("b1", s2[0] + [stages["a2"]], middle)
            go("c1+", [stages["b2+"]], pairs_out)
            go("b1+", s2[1] + [stages["a2+"]], middle)
            for k, end in enumerate(("", "+")):
                own[k] += [a1[k], stages["c1" + end], stages["b1" + end]]
        else:
            ring = range(far_count)
            for j in ring:
                for k, terms in enumerate(parts[j] if j > 0 else []):
                    own[k].append(
                        move_far(add(terms), [(i, (i + j) % far_count) for i in ring])
                    )
        return [sum(map(wide, terms)) for terms in own]

    def after(value, *others):
        return lax.optimization_barrier((value, *others))[0] if others else value

    def side_of(bit):
        return (red_at // bit) % 2

    here, few = 2 * mine // red_count, mine // red_count
    low = sum(side_of(bit) * (mine >> k) for k, bit in enumerate(bits) if k > 0)
    bases = [(owner * 2 + (near_at ^ side_of(1))) * mine + low for owner in owners]
    few_low = sum(side_of(bit) * (mine >> (k + 1)) for k, bit in enumerate(bits))
    end = at_end.astype(jnp.int32) if line else jnp.int32(0)
    base_at = 4 + len(bits)
    facts = [start, end, *map(side_of, bits), far_at, near_at, *bases, blk_at * mine + few_low]
    facts = jnp.stack(facts).astype(jnp.int32)

    def sum_rows(keep, got):
        for k, bit in enumerate(bits[1:]):
            keep, send = cut(3 + k, facts, keep, got)
            got = swap_red(send, bit)
        return keep, got

    def join_rows(value, which, *others):
        for k in reversed(which):
            got = after(swap_red(value, bits[k]), *others)
            value = join(2 + k, facts, value, got)
        return value

    head_at = blk_at // (blk_count // KV)
    one_head = lambda value: lax.dynamic_slice_in_dim(value, head_at * HD, HD, 1)
    cached = jnp.concatenate([one_head(cache_key), one_head(cache_value)], axis=1)

    token_at = (facts[base_at:-1, None] + jnp.arange(here, dtype=jnp.int32)).reshape(-1)
    few_at = facts[-1] + jnp.arange(few, dtype=jnp.int32)
    cosine, sine = tables(start + jnp.concatenate([token_at, few_at]))

    total_sq = jnp.sum(resid * resid, axis=1)
    for bit in bits:
        total_sq = total_sq + after(swap_red(total_sq, bit), facts)
    normed = (
        resid * lax.rsqrt(total_sq[:, None] / (width * red_count) + 1e-05) * norm_gain[None, :]
    ).astype(jnp.bfloat16)

    def pieces_of(value):
        return jnp.split(value, PIECES, axis=1)

    slots = range(far_count)
    last = far_count - 1
    hops = spread(normed)
    near = [swap_near(normed)]

    def ask(j, *others):
        return halves(facts, [after(far[j], *others), near[j]], [w_query])

    def have(*hops):
        return hops if line else ()

    def reduce(pair, got, *others):
        return sum_rows(after(pair[0], *others), got)

    def core(pair):
        return swap_red(pair[1], bits[0])

    half = mine // 2
    rest = range(1, len(bits))
    cached = after(cached, normed)[None]
    kv = halves(facts, [normed[:half], normed[half:]], [w_key, w_value])
    cached = join_rows(cached, rest, near[0], kv[0])
    cached = cached.reshape(red_count // 2, -1, 2 * HD)
    kv = reduce(kv, core(kv), near[0], hops[0], *have(hops[1]))
    shift = (blk_count // KV).bit_length() - 1
    same, other = pack(
        far_count * here, shift, base_at - 2, far_count, facts, *kv, cosine, sine
    )
    other = swap_near(other)
    far = [normed]
    asked = [ask(0, same, hops[0], *have(hops[1]))]
    far += arrive(hops, facts, asked[0][0])
    near += [swap_near(far[j]) for j in slots[1:]]
    moved = [core(asked[0])]
    keys, values = merge(facts, cached, after(swap_red(cached, bits[0]), asked[0][0]))
    fresh = jnp.stack([same, after(other, asked[0][0])], axis=1)
    fresh = [fresh[0]] + [
        move_far(fresh[d], [(k, k ^ d) for k in range(far_count)]) for d in range(1, far_count)
    ]
    asked.append(ask(1, keys, far[2], fresh[0], *have(hops[-1])))
    moved.append(core(asked[1]))
    fresh = lax.optimization_barrier((*fresh, asked[1][0]))[:-1]
    fresh = jnp.concatenate(fresh)
    asked[0] = reduce(asked[0], moved[0], asked[1][0])
    for j in range(2, last):
        asked.append(ask(j, asked[j - 2][0], far[j + 1], fresh))
        moved.append(core(asked[j]))
        if j < last - 1:
            asked[j - 1] = reduce(asked[j - 1], moved[j - 1], asked[j][0])
    rows = here * (w_query.shape[1] // HD)

    def mix(j, new, *others):
        keep, got = asked[j]
        old = [after(keep, *others), got, cosine, sine, keys, values]
        return attend(base_at, far_count, j, facts, here, rows, old, new)

    rest = range(1, len(bits))
    fresh = join_rows(fresh, rest, asked[last - 1][0])
    asked[last - 2] = reduce(asked[last - 2], moved[last - 2], fresh)
    begun = mix(0, None, asked[last - 2][0], fresh)
    fresh = join_rows(fresh, [0], begun[2]).reshape(blk_count * mine, 2 * HD)
    mixed = [None] * far_count
    mixed[0] = attend(base_at, far_count, 0, facts, here, rows, begun, fresh)
    asked.append(ask(last, mixed[0], asked[last - 2][1]))
    moved.append(core(asked[last]))

    parts = [None] * far_count
    per_half = red_count // 2
    turns = [
        sum(bit for i, bit in enumerate(bits[1:]) if k & (per_half >> (i + 1)))
        for k in range(per_half)
    ]
    turns = turns + [turn | bits[0] for turn in turns]

    def share(j):
        return [swap_red(mixed[j], turn) if turn else mixed[j] for turn in turns]

    def project(j, blocks, *others):
        blocks = [after(blocks[0], *others), *blocks[1:]]
        return halves(facts, blocks, [w_out])

    def finish(j, pair, *others):
        keep, send = pair
        send = after(send, *others)
        send = (send * SHRINK).astype(jnp.float16)
        send = [send] if j == 0 else pieces_of(send)
        got = [swap_near(p) for p in send]
        pieces = pieces_of(got[0]) if j == 0 else got
        parts[j] = [[p * SHRINK, g] for p, g in zip(pieces_of(keep), pieces)]
        return send, got

    shared = {0: share(0)}
    asked[last] = reduce(asked[last], moved[last])
    asked[last - 1] = reduce(asked[last - 1], moved[last - 1], asked[last][0])
    mixed[1] = mix(1, fresh, asked[last - 1][0])
    shared[1] = share(1)
    done, got = finish(0, project(0, shared[0], mixed[1], asked[last][1]))
    mixed[last] = mix(last, fresh, *done)
    shared[last] = share(last)
    done, got1 = finish(1, project(1, shared[1], mixed[last]))
    done = [*done, *got]
    for j in range(2, last):
        mixed[j] = mix(j, fresh, *done)
        shared[j] = share(j)
        done = [mixed[j]]
    first = [add(parts[1][0], *done)]
    first.append(add(parts[1][1], first[0]))
    done, _ = finish(last, project(last, shared[last], *done, *first))
    for j in range(2, last):
        done, _ = finish(j, project(j, shared[j], *done))
    return resid + jnp.concatenate(collect(parts, first), axis=1) * (1.0 / SHRINK)


def solution(mesh):
    placed = (
        P("blk", "red"),
        P("red"),
        P("red", "blk"),
        P("red", None),
        P("red", None),
        P("blk", "red"),
        P("red", None),
        P("red", None),
        P(),
    )
    return jax.shard_map(
        on_device, mesh=mesh, in_specs=placed, out_specs=P("blk", "red"), check_vma=False
    )
```

```python
import functools
import math

import jax
import jax.numpy as jnp
from jax import lax
from jax.experimental import pallas as pl
from jax.experimental.pallas import tpu as pltpu
from jax.sharding import PartitionSpec as P

KV = 8
HD = 128
THETA = 500000.0
LOW = -1e30
RATE = HD**-0.5 / math.log(2.0)
SHRINK = 1.0 / 32.0
MIB = 1024 * 1024
PIECES = 2
COST = pl.CostEstimate(flops=0, bytes_accessed=0, transcendentals=0)


def tables(positions):
    half = HD // 2
    steps = jnp.arange(half, dtype=jnp.float32)
    freq = THETA ** (-(steps * 2.0) / HD)
    angle = positions.astype(jnp.float32)[..., None] * freq
    cosine, sine = jnp.cos(angle), jnp.sin(angle)
    return (
        jnp.concatenate([cosine, cosine], axis=-1),
        jnp.concatenate([-sine, sine], axis=-1),
    )


def fold(parts, peak, acc):
    lanes = [score[:, at : at + HD] for score, _ in parts for at in range(0, score.shape[1], HD)]
    top = jnp.max(functools.reduce(jnp.maximum, lanes), axis=1, keepdims=True)
    new_peak = jnp.maximum(peak, top)
    carry = jnp.exp2((peak - new_peak) * RATE)
    acc = acc * jnp.concatenate([carry, carry], axis=1)
    for score, values in parts:
        shift = jnp.concatenate([new_peak] * (score.shape[1] // HD), axis=1)
        weights = jnp.exp2((score - shift) * RATE).astype(jnp.bfloat16)
        both = jnp.concatenate([values, jnp.ones(values.shape, values.dtype)], axis=1)
        acc = acc + jnp.dot(weights, both, preferred_element_type=jnp.float32)
    return new_peak, acc


def scores(query, keys):
    return lax.dot_general(
        query, keys, (((1,), (1,)), ((), ())), preferred_element_type=jnp.float32
    )


def attention_kernel(base_at, far_count, slot, unit, tile, cached, spanned, *refs):
    refs = list(refs)
    facts_ref = refs.pop(0)
    if cached:
        keep_ref, got_ref, cos_ref, sin_ref, key_ref, value_ref = refs[:6]
        refs = refs[6:]
    else:
        old_q_ref, old_peak_ref, old_acc_ref = refs[:3]
        refs = refs[3:]
    if spanned:
        fresh_ref, out_ref = refs[:2]
        refs = refs[2:]
    q_ref, peak_ref, acc_ref = refs if cached else (old_q_ref, old_peak_ref, old_acc_ref)
    start = facts_ref[0]
    rows_here = q_ref.shape[0]
    tiles = [slice(low, low + tile) for low in range(0, rows_here, tile)]

    def step(base, count, masked):
        for rows in tiles:
            parts = []
            for k in range(count):
                low = pl.multiple_of(base + k * unit, unit)
                here = pl.ds(low, unit)
                score = jnp.dot(
                    q_ref[rows, :], key_ref[:, here], preferred_element_type=jnp.float32
                )
                if masked and k == count - 1:
                    at = low + lax.broadcasted_iota(jnp.int32, (1, unit), 1)
                    score = jnp.where(at < start, score, LOW)
                parts.append((score, value_ref[here, :]))
            peak_ref[rows, :], acc_ref[rows, :] = fold(parts, peak_ref[rows, :], acc_ref[rows, :])

    if cached:
        tokens = keep_ref.shape[0]
        mine = slice(slot * tokens, (slot + 1) * tokens)
        cosine, sine = cos_ref[mine, :], sin_ref[mine, :]
        rotated = []
        for head in range(keep_ref.shape[1] // HD):
            at = slice(head * HD, (head + 1) * HD)
            raw = keep_ref[:, at] + got_ref[:, at]
            rotated.append(raw * cosine + pltpu.roll(raw, HD // 2, 1) * sine)
        q_ref[...] = jnp.concatenate(rotated, axis=0).astype(q_ref.dtype)
        peak_ref[...] = jnp.full(peak_ref.shape, LOW, jnp.float32)
        acc_ref[...] = jnp.zeros(acc_ref.shape, jnp.float32)
        pairs = start // (2 * unit)
        done = pairs * (2 * unit)

        @pl.loop(0, pairs)
        def _(index):
            step(index * (2 * unit), 2, False)

        @pl.when((start > done) & (start <= done + unit))
        def _():
            step(done, 1, True)

        @pl.when(start > done + unit)
        def _():
            step(done, 2, True)

    if spanned:
        tokens = out_ref.shape[0]
        keys, values = fresh_ref[:, :HD], fresh_ref[:, HD:]
        far, near = facts_ref[base_at - 2], facts_ref[base_at - 1]
        own = fresh_ref.shape[0] // (2 * far_count)
        in_block = lax.broadcasted_iota(jnp.int32, (1, own), 1)
        key_at = jnp.concatenate(
            [
                in_block + ((far ^ d) * 2 + (near ^ k)) * own
                for d in range(far_count)
                for k in range(2)
            ],
            axis=1,
        )
        query_at = facts_ref[base_at + slot] + lax.broadcasted_iota(jnp.int32, (tokens, 1), 0)
        query_at = jnp.concatenate([query_at] * (tile // tokens), axis=0)
        for rows in tiles:
            score = jnp.where(key_at <= query_at, scores(q_ref[rows, :], keys), LOW)
            _, acc = fold([(score, values)], peak_ref[rows, :], acc_ref[rows, :])
            mixed = (acc[:, :HD] / acc[:, HD:]).astype(out_ref.dtype)
            for part in range(tile // tokens):
                head = rows.start // tokens + part
                out_ref[:, head * HD : (head + 1) * HD] = mixed[
                    part * tokens : (part + 1) * tokens
                ]


def attend(base_at, far_count, slot, facts, tokens, rows, old, new):
    cached = len(old) == 6
    spanned = new is not None
    unit = min(1024, old[5].shape[0] // 2) if cached else 0
    tile = min(256, rows)
    vmem = pl.BlockSpec(memory_space=pltpu.VMEM)
    state = [
        ((rows, HD), jnp.bfloat16),
        ((rows, HD), jnp.float32),
        ((rows, 2 * HD), jnp.float32),
    ]
    if spanned:
        out_shape = jax.ShapeDtypeStruct((tokens, rows // tokens * HD), jnp.bfloat16)
    else:
        out_shape = tuple(jax.ShapeDtypeStruct(*one) for one in state)
    operands = [*old, *([new] if spanned else [])]
    return pl.pallas_call(
        functools.partial(attention_kernel, base_at, far_count, slot, unit, tile, cached, spanned),
        out_shape=out_shape,
        in_specs=[pl.BlockSpec(memory_space=pltpu.SMEM)] + [vmem] * len(operands),
        out_specs=vmem if spanned else (vmem,) * 3,
        scratch_shapes=[pltpu.VMEM(*one) for one in state] if cached and spanned else [],
        compiler_params=pltpu.CompilerParams(vmem_limit_bytes=(9 if cached else 5) * MIB),
        cost_estimate=pl.CostEstimate(
            flops=8 * rows * HD * (old[5].shape[0] + new.shape[0]) if cached and spanned else 0,
            bytes_accessed=0,
            transcendentals=0,
        ),
        name="attention",
    )(facts, *operands)


def small_call(kernel, name, out_shape, facts, *operands):
    vmem = pl.BlockSpec(memory_space=pltpu.VMEM)
    return pl.pallas_call(
        kernel,
        out_shape=out_shape,
        in_specs=[pl.BlockSpec(memory_space=pltpu.SMEM)] + [vmem] * len(operands),
        out_specs=jax.tree.map(lambda _: vmem, out_shape),
        compiler_params=pltpu.CompilerParams(vmem_limit_bytes=4 * MIB),
        cost_estimate=COST,
        name=name,
    )(facts, *operands)


def cut_kernel(fact, facts_ref, keep_ref, got_ref, mine_ref, send_ref):
    half = mine_ref.shape[0]
    upper = facts_ref[fact] == 1
    low, high = (keep_ref[at, :] + got_ref[at, :] for at in (slice(0, half), slice(half, None)))
    mine_ref[...] = jnp.where(upper, high, low)
    send_ref[...] = jnp.where(upper, low, high)


def cut(fact, facts, keep, got):
    out = jax.ShapeDtypeStruct((keep.shape[0] // 2, keep.shape[1]), keep.dtype)
    return small_call(functools.partial(cut_kernel, fact), "cut", (out, out), facts, keep, got)


def join_kernel(fact, facts_ref, own_ref, got_ref, out_ref):
    half = own_ref.shape[1]
    upper = facts_ref[fact] == 1

    @pl.when(upper)
    def _():
        out_ref[:, :half] = got_ref[...]
        out_ref[:, half:] = own_ref[...]

    @pl.when(jnp.logical_not(upper))
    def _():
        out_ref[:, :half] = own_ref[...]
        out_ref[:, half:] = got_ref[...]


def join(fact, facts, own, got):
    count, half, width = own.shape
    if half % 16:
        upper = facts[fact] == 1
        return jnp.where(
            upper, jnp.concatenate([got, own], axis=1), jnp.concatenate([own, got], axis=1)
        )
    out = jax.ShapeDtypeStruct((count, 2 * half, width), own.dtype)
    return small_call(functools.partial(join_kernel, fact), "join", out, facts, own, got)


def merge_kernel(facts_ref, own_ref, got_ref, key_ref, value_ref):
    count, rows, _ = own_ref.shape
    for side in range(2):

        @pl.when(facts_ref[2] == side)
        def _():
            for k in range(count):
                for at, ref in ((2 * k + side, own_ref), (2 * k + 1 - side, got_ref)):
                    here = slice(at * rows, (at + 1) * rows)
                    key_ref[:, here] = ref[k, :, :HD].astype(jnp.float32).T.astype(key_ref.dtype)
                    value_ref[here, :] = ref[k, :, HD:]


def merge(facts, own, got):
    slots = 2 * own.shape[0] * own.shape[1]
    out = (
        jax.ShapeDtypeStruct((HD, slots), own.dtype),
        jax.ShapeDtypeStruct((slots, HD), own.dtype),
    )
    return small_call(merge_kernel, "merge", out, facts, own, got)


def pick_kernel(facts_ref, a_ref, b_ref, out_ref):
    @pl.when(facts_ref[1] == 1)
    def _():
        out_ref[...] = a_ref[...]

    @pl.when(facts_ref[1] != 1)
    def _():
        out_ref[...] = b_ref[...]


def pick(facts, a, b):
    return small_call(pick_kernel, "pick", jax.ShapeDtypeStruct(a.shape, a.dtype), facts, a, b)


def halves_kernel(blocks, tile, facts_ref, *refs):
    lhs, refs = refs[:blocks], refs[blocks:]
    w_refs, (keep_ref, send_ref) = refs[:-2], refs[-2:]
    rows, per_half = lhs[0].shape[0], blocks // 2
    upper, place = facts_ref[2] == 1, facts_ref[2] * 0
    for k in range(per_half.bit_length() - 1):
        place = place + facts_ref[3 + k] * (per_half >> (k + 1))
    both = jnp.concatenate([ref[...] for ref in lhs], axis=0)
    low = 0
    for w_ref in w_refs:

        @pl.loop(0, w_ref.shape[1] // tile)
        def _(step, low=low, w_ref=w_ref):
            at = pl.multiple_of(step * tile, tile)
            out = jnp.dot(both, w_ref[:, pl.ds(at, tile)], preferred_element_type=jnp.float32)
            here = pl.ds(pl.multiple_of(low + at, tile), tile)
            half = per_half * rows
            first = jnp.where(upper, out[half:], out[:half])
            second = jnp.where(upper, out[:half], out[half:])
            for k in range(per_half):
                to = pl.ds(pl.multiple_of((place ^ k) * rows, rows), rows)
                keep_ref[to, here] = first[k * rows : (k + 1) * rows]
                send_ref[to, here] = second[k * rows : (k + 1) * rows]

        low += w_ref.shape[1]


def halves(facts, lhs, weights):
    rows = lhs[0].shape[0] * len(lhs) // 2
    width = sum(w.shape[1] for w in weights)
    out = jax.ShapeDtypeStruct((rows, width), jnp.float32)
    vmem = pl.BlockSpec(memory_space=pltpu.VMEM)
    operands = [*lhs, *weights]
    return pl.pallas_call(
        functools.partial(halves_kernel, len(lhs), min(512, weights[0].shape[1])),
        out_shape=(out, out),
        in_specs=[pl.BlockSpec(memory_space=pltpu.SMEM)] + [vmem] * len(operands),
        out_specs=(vmem, vmem),
        compiler_params=pltpu.CompilerParams(vmem_limit_bytes=5 * MIB),
        cost_estimate=pl.CostEstimate(
            flops=4 * rows * weights[0].shape[0] * width, bytes_accessed=0, transcendentals=0
        ),
        name="halves",
    )(facts, *operands)


def pack_kernel(low, shift, where_at, facts_ref, keep_ref, got_ref, cos_ref, sin_ref, same_ref, other_ref):
    few = keep_ref.shape[0]
    cosine, sine = cos_ref[low : low + few, :], sin_ref[low : low + few, :]
    far, near = facts_ref[where_at], facts_ref[where_at + 1]
    for d in range(same_ref.shape[0]):
        for k, out_ref in enumerate((same_ref, other_ref)):
            head = ((far ^ d) * 2 + (near ^ k)) >> shift
            raw, value = (
                keep_ref[:, pl.ds(pl.multiple_of(at * HD, HD), HD)]
                + got_ref[:, pl.ds(pl.multiple_of(at * HD, HD), HD)]
                for at in (head, KV + head)
            )
            both = [raw * cosine + pltpu.roll(raw, HD // 2, 1) * sine, value]
            out_ref[d] = jnp.concatenate(both, axis=1).astype(out_ref.dtype)


def pack(low, shift, where_at, count, facts, keep, got, cosine, sine):
    out = jax.ShapeDtypeStruct((count, keep.shape[0], 2 * HD), jnp.bfloat16)
    kernel = functools.partial(pack_kernel, low, shift, where_at)
    return small_call(kernel, "pack", (out, out), facts, keep, got, cosine, sine)


def on_device(resid, norm_gain, w_query, w_key, w_value, w_out, cache_key, cache_value, prefix_len):
    blk_count, red_count = lax.axis_size("blk"), lax.axis_size("red")
    blk_at, red_at = lax.axis_index("blk"), lax.axis_index("red")
    start = prefix_len[0]
    mine, width = resid.shape
    far_count = blk_count // 2
    far_at, near_at = blk_at // 2, blk_at % 2
    bits = [1 << k for k in range(red_count.bit_length() - 1)]

    def swap_red(value, bit):
        return lax.ppermute(value, "red", [(k, k ^ bit) for k in range(red_count)])

    def swap_near(value):
        return lax.ppermute(value, "blk", [(k, k ^ 1) for k in range(blk_count)])

    def move_far(value, pairs):
        pairs = [(2 * a + k, 2 * b + k) for a, b in pairs for k in range(2)]
        return lax.ppermute(value, "blk", pairs)

    line = far_count == 4
    if line:
        at_end = (far_at == 0) | (far_at == 3)
        pairs_out = [(1, 0), (2, 3)]
        pairs_in = [(0, 1), (3, 2)]
        middle = [(1, 2), (2, 1)]
        owners = [
            far_at,
            far_at ^ 1,
            far_at ^ jnp.where(at_end, 2, 3),
            far_at ^ jnp.where(at_end, 3, 2),
        ]
    else:
        owners = [(far_at + j) % far_count for j in range(far_count)]

    def spread(own):
        if not line:
            ring = range(far_count)
            return [move_far(own, [((k + j) % far_count, k) for k in ring]) for j in ring if j > 0]
        a1 = move_far(own, pairs_out + pairs_in)
        b1 = move_far(own, middle)
        return [a1, b1, move_far(b1, pairs_out), move_far(a1, middle)]

    def arrive(hops, facts, *others):
        if not line:
            return hops
        a1, b1, a2, b2 = hops
        a3 = move_far(after(b2, *others), pairs_out)
        return [a1, pick(facts, a2, b1), pick(facts, a3, b2)]

    wide = lambda value: value.astype(jnp.float32)

    def add(terms, *others):
        return sum(map(wide, [*terms[:-1], after(terms[-1], *others)])).astype(jnp.float16)

    def collect(parts, passed):
        own = [list(terms) for terms in parts[0]]
        if line:
            s2, s3 = parts[2:]
            last = passed[-1]
            stages = {}

            def go(name, terms, pairs):
                nonlocal last
                last = add(terms, last)
                stages[name] = move_far(last, pairs)

            go("a3", s3[0], pairs_in)
            go("a3+", s3[1], pairs_in)
            go("b2", s3[0] + [stages["a3"]], middle)
            go("a2", s2[0], pairs_in)
            go("b2+", s3[1] + [stages["a3+"]], middle)
            go("c1", [stages["b2"]], pairs_out)
            go("a2+", s2[1], pairs_in)
            go("b1", s2[0] + [stages["a2"]], middle)
            go("c1+", [stages["b2+"]], pairs_out)
            go("b1+", s2[1] + [stages["a2+"]], middle)
            for k, end in enumerate(("", "+")):
                own[k] += [passed[k], stages["c1" + end], stages["b1" + end]]
        else:
            ring = range(far_count)
            for j in ring:
                for k, terms in enumerate(parts[j] if j > 0 else []):
                    own[k].append(
                        move_far(add(terms), [(i, (i + j) % far_count) for i in ring])
                    )
        return [sum(map(wide, terms)) for terms in own]

    def after(value, *others):
        return lax.optimization_barrier((value, *others))[0] if others else value

    def side_of(bit):
        return (red_at // bit) % 2

    here, few = 2 * mine // red_count, mine // red_count
    low = sum(side_of(bit) * (mine >> k) for k, bit in enumerate(bits) if k > 0)
    bases = [(owner * 2 + (near_at ^ side_of(1))) * mine + low for owner in owners]
    few_low = sum(side_of(bit) * (mine >> (k + 1)) for k, bit in enumerate(bits))
    end = at_end.astype(jnp.int32) if line else jnp.int32(0)
    base_at = 4 + len(bits)
    facts = [start, end, *map(side_of, bits), far_at, near_at, *bases, blk_at * mine + few_low]
    facts = jnp.stack(facts).astype(jnp.int32)

    def sum_rows(keep, got):
        for k, bit in enumerate(bits[1:]):
            keep, send = cut(3 + k, facts, keep, got)
            got = swap_red(send, bit)
        return keep, got

    def join_rows(value, which, *others):
        for k in reversed(which):
            got = after(swap_red(value, bits[k]), *others)
            value = join(2 + k, facts, value, got)
        return value

    head_at = blk_at // (blk_count // KV)
    one_head = lambda value: lax.dynamic_slice_in_dim(value, head_at * HD, HD, 1)
    cached = jnp.concatenate([one_head(cache_key), one_head(cache_value)], axis=1)

    token_at = (facts[base_at:-1, None] + jnp.arange(here, dtype=jnp.int32)).reshape(-1)
    few_at = facts[-1] + jnp.arange(few, dtype=jnp.int32)
    cosine, sine = tables(start + jnp.concatenate([token_at, few_at]))

    total_sq = jnp.sum(resid * resid, axis=1)
    for bit in bits:
        total_sq = total_sq + after(swap_red(total_sq, bit), facts)
    normed = (
        resid * lax.rsqrt(total_sq[:, None] / (width * red_count) + 1e-05) * norm_gain[None, :]
    ).astype(jnp.bfloat16)

    def pieces_of(value):
        return jnp.split(value, PIECES, axis=1)

    slots = range(far_count)
    last = far_count - 1
    hops = spread(normed)
    near = [swap_near(normed)]

    def ask(j, *others):
        return halves(facts, [after(far[j], *others), near[j]], [w_query])

    def have(*hops):
        return hops if line else ()

    def reduce(pair, got, *others):
        return sum_rows(after(pair[0], *others), got)

    def core(pair):
        return swap_red(pair[1], bits[0])

    half = mine // 2
    rest = range(1, len(bits))
    cached = after(cached, normed)[None]
    kv = halves(facts, [normed[:half], normed[half:]], [w_key, w_value])
    kv = reduce(kv, core(kv), near[0], hops[0], *have(hops[1]))
    cached = join_rows(cached, rest, kv[0])
    cached = cached.reshape(red_count // 2, -1, 2 * HD)
    shift = (blk_count // KV).bit_length() - 1
    same, other = pack(
        far_count * here, shift, base_at - 2, far_count, facts, *kv, cosine, sine
    )
    other = swap_near(other)
    far = [normed]
    asked = [ask(0, same, hops[0], *have(hops[1]))]
    far += arrive(hops, facts, asked[0][0])
    near += [swap_near(far[j]) for j in slots[1:]]
    moved = [core(asked[0])]
    keys, values = merge(facts, cached, after(swap_red(cached, bits[0]), asked[0][0]))
    fresh = jnp.stack([same, after(other, asked[0][0])], axis=1)
    held, bit = [fresh[d] for d in range(far_count)], 1

    def double(held, bit):
        send = jnp.concatenate(held[1::2])
        got = move_far(send, [(k, k ^ bit) for k in range(far_count)])
        return held[::2], got

    def settle(held, got):
        return [
            jnp.concatenate([one, part])
            for one, part in zip(held, jnp.split(got, len(held)))
        ]

    got = other
    while len(held) > 2:
        held, got = double(held, bit)
        held = settle(held, got)
        bit *= 2
    stage = got
    held, got = double(held, bit)
    asked.append(ask(1, keys, far[2], stage, *have(hops[-1])))
    moved.append(core(asked[1]))
    fresh = settle(held, after(got, asked[1][0]))[0]
    asked[0] = reduce(asked[0], moved[0], asked[1][0])
    for j in range(2, last):
        asked.append(ask(j, asked[j - 2][0], far[j + 1], fresh))
        moved.append(core(asked[j]))
        if j < last - 1:
            asked[j - 1] = reduce(asked[j - 1], moved[j - 1], asked[j][0])
    rows = here * (w_query.shape[1] // HD)

    def mix(j, new, *others):
        keep, got = asked[j]
        old = [after(keep, *others), got, cosine, sine, keys, values]
        return attend(base_at, far_count, j, facts, here, rows, old, new)

    rest = range(1, len(bits))
    fresh = join_rows(fresh, rest, asked[last - 1][0])
    asked[last - 2] = reduce(asked[last - 2], moved[last - 2], fresh)
    begun = mix(0, None, asked[last - 2][0], fresh)
    fresh = join_rows(fresh, [0], begun[2]).reshape(blk_count * mine, 2 * HD)
    mixed = [None] * far_count
    mixed[0] = attend(base_at, far_count, 0, facts, here, rows, begun, fresh)
    asked.append(ask(last, mixed[0], asked[last - 2][1]))
    moved.append(core(asked[last]))

    parts = [None] * far_count
    per_half = red_count // 2
    turns = [
        sum(bit for i, bit in enumerate(bits[1:]) if k & (per_half >> (i + 1)))
        for k in range(per_half)
    ]
    turns = turns + [turn | bits[0] for turn in turns]

    def share(j):
        return [swap_red(mixed[j], turn) if turn else mixed[j] for turn in turns]

    def project(j, blocks, *others):
        blocks = [after(blocks[0], *others), *blocks[1:]]
        return halves(facts, blocks, [w_out])

    def finish(j, pair, *others):
        keep, send = pair
        send = after(send, *others)
        send = (send * SHRINK).astype(jnp.float16)
        send = [send] if j == 0 else pieces_of(send)
        got = [swap_near(p) for p in send]
        pieces = pieces_of(got[0]) if j == 0 else got
        parts[j] = [[p * SHRINK, g] for p, g in zip(pieces_of(keep), pieces)]
        return send, got

    shared = {0: share(0)}
    asked[last] = reduce(asked[last], moved[last])
    asked[last - 1] = reduce(asked[last - 1], moved[last - 1], asked[last][0])
    mixed[1] = mix(1, fresh, asked[last - 1][0])
    shared[1] = share(1)
    done, got = finish(0, project(0, shared[0], mixed[1], asked[last][1]))
    mixed[last] = mix(last, fresh, *done)
    shared[last] = share(last)
    done, got1 = finish(1, project(1, shared[1], mixed[last]))
    done = [*done, *got]
    for j in range(2, last):
        mixed[j] = mix(j, fresh, *done)
        shared[j] = share(j)
        done = [mixed[j]]
    first = [add(parts[1][0], *done)]
    hop = [(k, k ^ 1) for k in range(far_count)]
    passed = [move_far(first[0], hop)]
    done, _ = finish(last, project(last, shared[last], *done, first[0]))
    first.append(add(parts[1][1], *done))
    passed.append(move_far(first[1], hop))
    done = [*done, first[1], passed[0]]
    for j in range(2, last):
        done, _ = finish(j, project(j, shared[j], *done))
    return resid + jnp.concatenate(collect(parts, passed), axis=1) * (1.0 / SHRINK)


def solution(mesh):
    placed = (
        P("blk", "red"),
        P("red"),
        P("red", "blk"),
        P("red", None),
        P("red", None),
        P("blk", "red"),
        P("red", None),
        P("red", None),
        P(),
    )
    return jax.shard_map(
        on_device, mesh=mesh, in_specs=placed, out_specs=P("blk", "red"), check_vma=False
    )
```

```python
import functools
import math

import jax
import jax.numpy as jnp
from jax import lax
from jax.experimental import pallas as pl
from jax.experimental.pallas import tpu as pltpu
from jax.sharding import PartitionSpec as P

KV = 8
HD = 128
THETA = 500000.0
LOW = -1e30
RATE = HD**-0.5 / math.log(2.0)
SHRINK = 1.0 / 32.0
MIB = 1024 * 1024
PIECES = 2
COST = pl.CostEstimate(flops=0, bytes_accessed=0, transcendentals=0)


def tables(positions):
    half = HD // 2
    steps = jnp.arange(half, dtype=jnp.float32)
    freq = THETA ** (-(steps * 2.0) / HD)
    angle = positions.astype(jnp.float32)[..., None] * freq
    cosine, sine = jnp.cos(angle), jnp.sin(angle)
    return (
        jnp.concatenate([cosine, cosine], axis=-1),
        jnp.concatenate([-sine, sine], axis=-1),
    )


def fold(parts, peak, acc):
    lanes = [score[:, at : at + HD] for score, _ in parts for at in range(0, score.shape[1], HD)]
    top = jnp.max(functools.reduce(jnp.maximum, lanes), axis=1, keepdims=True)
    new_peak = jnp.maximum(peak, top)
    carry = jnp.exp2((peak - new_peak) * RATE)
    acc = acc * jnp.concatenate([carry, carry], axis=1)
    for score, values in parts:
        shift = jnp.concatenate([new_peak] * (score.shape[1] // HD), axis=1)
        weights = jnp.exp2((score - shift) * RATE).astype(jnp.bfloat16)
        both = jnp.concatenate([values, jnp.ones(values.shape, values.dtype)], axis=1)
        acc = acc + jnp.dot(weights, both, preferred_element_type=jnp.float32)
    return new_peak, acc


def scores(query, keys):
    return lax.dot_general(
        query, keys, (((1,), (1,)), ((), ())), preferred_element_type=jnp.float32
    )


def attention_kernel(base_at, far_count, slot, unit, tile, cached, spanned, *refs):
    refs = list(refs)
    facts_ref = refs.pop(0)
    if cached:
        keep_ref, got_ref, cos_ref, sin_ref, key_ref, value_ref = refs[:6]
        refs = refs[6:]
    else:
        old_q_ref, old_peak_ref, old_acc_ref = refs[:3]
        refs = refs[3:]
    if spanned:
        fresh_ref, out_ref = refs[:2]
        refs = refs[2:]
    q_ref, peak_ref, acc_ref = refs if cached else (old_q_ref, old_peak_ref, old_acc_ref)
    start = facts_ref[0]
    rows_here = q_ref.shape[0]
    tiles = [slice(low, low + tile) for low in range(0, rows_here, tile)]

    def step(base, count, masked):
        for rows in tiles:
            parts = []
            for k in range(count):
                low = pl.multiple_of(base + k * unit, unit)
                here = pl.ds(low, unit)
                score = jnp.dot(
                    q_ref[rows, :], key_ref[:, here], preferred_element_type=jnp.float32
                )
                if masked and k == count - 1:
                    at = low + lax.broadcasted_iota(jnp.int32, (1, unit), 1)
                    score = jnp.where(at < start, score, LOW)
                parts.append((score, value_ref[here, :]))
            peak_ref[rows, :], acc_ref[rows, :] = fold(parts, peak_ref[rows, :], acc_ref[rows, :])

    if cached:
        tokens = keep_ref.shape[0]
        mine = slice(slot * tokens, (slot + 1) * tokens)
        cosine, sine = cos_ref[mine, :], sin_ref[mine, :]
        rotated = []
        for head in range(keep_ref.shape[1] // HD):
            at = slice(head * HD, (head + 1) * HD)
            raw = keep_ref[:, at] + got_ref[:, at]
            rotated.append(raw * cosine + pltpu.roll(raw, HD // 2, 1) * sine)
        q_ref[...] = jnp.concatenate(rotated, axis=0).astype(q_ref.dtype)
        peak_ref[...] = jnp.full(peak_ref.shape, LOW, jnp.float32)
        acc_ref[...] = jnp.zeros(acc_ref.shape, jnp.float32)
        pairs = start // (2 * unit)
        done = pairs * (2 * unit)

        @pl.loop(0, pairs)
        def _(index):
            step(index * (2 * unit), 2, False)

        @pl.when((start > done) & (start <= done + unit))
        def _():
            step(done, 1, True)

        @pl.when(start > done + unit)
        def _():
            step(done, 2, True)

    if spanned:
        tokens = out_ref.shape[0]
        keys, values = fresh_ref[:, :HD], fresh_ref[:, HD:]
        far, near = facts_ref[base_at - 2], facts_ref[base_at - 1]
        own = fresh_ref.shape[0] // (2 * far_count)
        in_block = lax.broadcasted_iota(jnp.int32, (1, own), 1)
        key_at = jnp.concatenate(
            [
                in_block + ((far ^ d) * 2 + (near ^ k)) * own
                for d in range(far_count)
                for k in range(2)
            ],
            axis=1,
        )
        query_at = facts_ref[base_at + slot] + lax.broadcasted_iota(jnp.int32, (tokens, 1), 0)
        query_at = jnp.concatenate([query_at] * (tile // tokens), axis=0)
        for rows in tiles:
            score = jnp.where(key_at <= query_at, scores(q_ref[rows, :], keys), LOW)
            _, acc = fold([(score, values)], peak_ref[rows, :], acc_ref[rows, :])
            mixed = (acc[:, :HD] / acc[:, HD:]).astype(out_ref.dtype)
            for part in range(tile // tokens):
                head = rows.start // tokens + part
                out_ref[:, head * HD : (head + 1) * HD] = mixed[
                    part * tokens : (part + 1) * tokens
                ]


def attend(base_at, far_count, slot, facts, tokens, rows, old, new):
    cached = len(old) == 6
    spanned = new is not None
    unit = min(1024, old[5].shape[0] // 2) if cached else 0
    tile = min(256, rows)
    vmem = pl.BlockSpec(memory_space=pltpu.VMEM)
    state = [
        ((rows, HD), jnp.bfloat16),
        ((rows, HD), jnp.float32),
        ((rows, 2 * HD), jnp.float32),
    ]
    if spanned:
        out_shape = jax.ShapeDtypeStruct((tokens, rows // tokens * HD), jnp.bfloat16)
    else:
        out_shape = tuple(jax.ShapeDtypeStruct(*one) for one in state)
    operands = [*old, *([new] if spanned else [])]
    return pl.pallas_call(
        functools.partial(attention_kernel, base_at, far_count, slot, unit, tile, cached, spanned),
        out_shape=out_shape,
        in_specs=[pl.BlockSpec(memory_space=pltpu.SMEM)] + [vmem] * len(operands),
        out_specs=vmem if spanned else (vmem,) * 3,
        scratch_shapes=[pltpu.VMEM(*one) for one in state] if cached and spanned else [],
        compiler_params=pltpu.CompilerParams(vmem_limit_bytes=(9 if cached else 5) * MIB),
        cost_estimate=pl.CostEstimate(
            flops=8 * rows * HD * (old[5].shape[0] + new.shape[0]) if cached and spanned else 0,
            bytes_accessed=0,
            transcendentals=0,
        ),
        name="attention",
    )(facts, *operands)


def small_call(kernel, name, out_shape, facts, *operands):
    vmem = pl.BlockSpec(memory_space=pltpu.VMEM)
    return pl.pallas_call(
        kernel,
        out_shape=out_shape,
        in_specs=[pl.BlockSpec(memory_space=pltpu.SMEM)] + [vmem] * len(operands),
        out_specs=jax.tree.map(lambda _: vmem, out_shape),
        compiler_params=pltpu.CompilerParams(vmem_limit_bytes=4 * MIB),
        cost_estimate=COST,
        name=name,
    )(facts, *operands)


def cut_kernel(fact, facts_ref, keep_ref, got_ref, mine_ref, send_ref):
    half = mine_ref.shape[0]
    upper = facts_ref[fact] == 1
    low, high = (keep_ref[at, :] + got_ref[at, :] for at in (slice(0, half), slice(half, None)))
    mine_ref[...] = jnp.where(upper, high, low)
    send_ref[...] = jnp.where(upper, low, high)


def cut(fact, facts, keep, got):
    out = jax.ShapeDtypeStruct((keep.shape[0] // 2, keep.shape[1]), keep.dtype)
    return small_call(functools.partial(cut_kernel, fact), "cut", (out, out), facts, keep, got)


def join_kernel(fact, facts_ref, own_ref, got_ref, out_ref):
    half = own_ref.shape[1]
    upper = facts_ref[fact] == 1

    @pl.when(upper)
    def _():
        out_ref[:, :half] = got_ref[...]
        out_ref[:, half:] = own_ref[...]

    @pl.when(jnp.logical_not(upper))
    def _():
        out_ref[:, :half] = own_ref[...]
        out_ref[:, half:] = got_ref[...]


def join(fact, facts, own, got):
    count, half, width = own.shape
    if half % 16:
        upper = facts[fact] == 1
        return jnp.where(
            upper, jnp.concatenate([got, own], axis=1), jnp.concatenate([own, got], axis=1)
        )
    out = jax.ShapeDtypeStruct((count, 2 * half, width), own.dtype)
    return small_call(functools.partial(join_kernel, fact), "join", out, facts, own, got)


def merge_kernel(facts_ref, own_ref, got_ref, key_ref, value_ref):
    count, rows, _ = own_ref.shape
    for side in range(2):

        @pl.when(facts_ref[2] == side)
        def _():
            for k in range(count):
                for at, ref in ((2 * k + side, own_ref), (2 * k + 1 - side, got_ref)):
                    here = slice(at * rows, (at + 1) * rows)
                    key_ref[:, here] = ref[k, :, :HD].astype(jnp.float32).T.astype(key_ref.dtype)
                    value_ref[here, :] = ref[k, :, HD:]


def merge(facts, own, got):
    slots = 2 * own.shape[0] * own.shape[1]
    out = (
        jax.ShapeDtypeStruct((HD, slots), own.dtype),
        jax.ShapeDtypeStruct((slots, HD), own.dtype),
    )
    return small_call(merge_kernel, "merge", out, facts, own, got)


def pick_kernel(facts_ref, a_ref, b_ref, out_ref):
    @pl.when(facts_ref[1] == 1)
    def _():
        out_ref[...] = a_ref[...]

    @pl.when(facts_ref[1] != 1)
    def _():
        out_ref[...] = b_ref[...]


def pick(facts, a, b):
    return small_call(pick_kernel, "pick", jax.ShapeDtypeStruct(a.shape, a.dtype), facts, a, b)


def halves_kernel(blocks, tile, facts_ref, *refs):
    lhs, refs = refs[:blocks], refs[blocks:]
    w_refs, (keep_ref, send_ref) = refs[:-2], refs[-2:]
    rows, per_half = lhs[0].shape[0], blocks // 2
    upper, place = facts_ref[2] == 1, facts_ref[2] * 0
    for k in range(per_half.bit_length() - 1):
        place = place + facts_ref[3 + k] * (per_half >> (k + 1))
    both = jnp.concatenate([ref[...] for ref in lhs], axis=0)
    low = 0
    for w_ref in w_refs:

        @pl.loop(0, w_ref.shape[1] // tile)
        def _(step, low=low, w_ref=w_ref):
            at = pl.multiple_of(step * tile, tile)
            out = jnp.dot(both, w_ref[:, pl.ds(at, tile)], preferred_element_type=jnp.float32)
            here = pl.ds(pl.multiple_of(low + at, tile), tile)
            half = per_half * rows
            first = jnp.where(upper, out[half:], out[:half])
            second = jnp.where(upper, out[:half], out[half:])
            for k in range(per_half):
                to = pl.ds(pl.multiple_of((place ^ k) * rows, rows), rows)
                keep_ref[to, here] = first[k * rows : (k + 1) * rows]
                send_ref[to, here] = second[k * rows : (k + 1) * rows]

        low += w_ref.shape[1]


def halves(facts, lhs, weights):
    rows = lhs[0].shape[0] * len(lhs) // 2
    width = sum(w.shape[1] for w in weights)
    out = jax.ShapeDtypeStruct((rows, width), jnp.float32)
    vmem = pl.BlockSpec(memory_space=pltpu.VMEM)
    operands = [*lhs, *weights]
    return pl.pallas_call(
        functools.partial(halves_kernel, len(lhs), min(512, weights[0].shape[1])),
        out_shape=(out, out),
        in_specs=[pl.BlockSpec(memory_space=pltpu.SMEM)] + [vmem] * len(operands),
        out_specs=(vmem, vmem),
        compiler_params=pltpu.CompilerParams(vmem_limit_bytes=5 * MIB),
        cost_estimate=pl.CostEstimate(
            flops=4 * rows * weights[0].shape[0] * width, bytes_accessed=0, transcendentals=0
        ),
        name="halves",
    )(facts, *operands)


def pack_kernel(low, shift, where_at, facts_ref, keep_ref, got_ref, cos_ref, sin_ref, same_ref, other_ref):
    few = keep_ref.shape[0]
    cosine, sine = cos_ref[low : low + few, :], sin_ref[low : low + few, :]
    far, near = facts_ref[where_at], facts_ref[where_at + 1]
    for d in range(same_ref.shape[0]):
        for k, out_ref in enumerate((same_ref, other_ref)):
            head = ((far ^ d) * 2 + (near ^ k)) >> shift
            raw, value = (
                keep_ref[:, pl.ds(pl.multiple_of(at * HD, HD), HD)]
                + got_ref[:, pl.ds(pl.multiple_of(at * HD, HD), HD)]
                for at in (head, KV + head)
            )
            both = [raw * cosine + pltpu.roll(raw, HD // 2, 1) * sine, value]
            out_ref[d] = jnp.concatenate(both, axis=1).astype(out_ref.dtype)


def pack(low, shift, where_at, count, facts, keep, got, cosine, sine):
    out = jax.ShapeDtypeStruct((count, keep.shape[0], 2 * HD), jnp.bfloat16)
    kernel = functools.partial(pack_kernel, low, shift, where_at)
    return small_call(kernel, "pack", (out, out), facts, keep, got, cosine, sine)


def on_device(resid, norm_gain, w_query, w_key, w_value, w_out, cache_key, cache_value, prefix_len):
    blk_count, red_count = lax.axis_size("blk"), lax.axis_size("red")
    blk_at, red_at = lax.axis_index("blk"), lax.axis_index("red")
    start = prefix_len[0]
    mine, width = resid.shape
    far_count = blk_count // 2
    far_at, near_at = blk_at // 2, blk_at % 2
    bits = [1 << k for k in range(red_count.bit_length() - 1)]

    def swap_red(value, bit):
        return lax.ppermute(value, "red", [(k, k ^ bit) for k in range(red_count)])

    def swap_near(value):
        return lax.ppermute(value, "blk", [(k, k ^ 1) for k in range(blk_count)])

    def move_far(value, pairs):
        pairs = [(2 * a + k, 2 * b + k) for a, b in pairs for k in range(2)]
        return lax.ppermute(value, "blk", pairs)

    line = far_count == 4
    if line:
        at_end = (far_at == 0) | (far_at == 3)
        pairs_out = [(1, 0), (2, 3)]
        pairs_in = [(0, 1), (3, 2)]
        middle = [(1, 2), (2, 1)]
        owners = [
            far_at,
            far_at ^ 1,
            far_at ^ jnp.where(at_end, 2, 3),
            far_at ^ jnp.where(at_end, 3, 2),
        ]
    else:
        owners = [(far_at + j) % far_count for j in range(far_count)]

    def spread(own):
        if not line:
            ring = range(far_count)
            return [move_far(own, [((k + j) % far_count, k) for k in ring]) for j in ring if j > 0]
        a1 = move_far(own, pairs_out + pairs_in)
        b1 = move_far(own, middle)
        return [a1, b1, move_far(b1, pairs_out), move_far(a1, middle)]

    def arrive(hops, facts, *others):
        if not line:
            return hops
        a1, b1, a2, b2 = hops
        a3 = move_far(after(b2, *others), pairs_out)
        return [a1, pick(facts, a2, b1), pick(facts, a3, b2)]

    wide = lambda value: value.astype(jnp.float32)

    def add(terms, *others):
        return sum(map(wide, [*terms[:-1], after(terms[-1], *others)])).astype(jnp.float16)

    def collect(parts, passed, first):
        own = [list(terms) for terms in parts[0]]
        if line:
            s2, s3 = parts[2:]
            last = first
            stages = {}

            def go(name, terms, pairs, *others):
                nonlocal last
                last = add(terms, last, *others)
                stages[name] = move_far(last, pairs)

            go("a3", s3[0], pairs_in)
            go("a3+", s3[1], pairs_in)
            go("b2", s3[0] + [stages["a3"]], middle, passed[0])
            go("a2", s2[0], pairs_in)
            go("b2+", s3[1] + [stages["a3+"]], middle, passed[1])
            go("c1", [stages["b2"]], pairs_out)
            go("a2+", s2[1], pairs_in)
            go("b1", s2[0] + [stages["a2"]], middle)
            go("c1+", [stages["b2+"]], pairs_out)
            go("b1+", s2[1] + [stages["a2+"]], middle)
            for k, end in enumerate(("", "+")):
                own[k] += [passed[k], stages["c1" + end], stages["b1" + end]]
        else:
            ring = range(far_count)
            for j in ring:
                for k, terms in enumerate(parts[j] if j > 0 else []):
                    own[k].append(
                        move_far(add(terms), [(i, (i + j) % far_count) for i in ring])
                    )
        return [sum(map(wide, terms)) for terms in own]

    def after(value, *others):
        return lax.optimization_barrier((value, *others))[0] if others else value

    def side_of(bit):
        return (red_at // bit) % 2

    here, few = 2 * mine // red_count, mine // red_count
    low = sum(side_of(bit) * (mine >> k) for k, bit in enumerate(bits) if k > 0)
    bases = [(owner * 2 + (near_at ^ side_of(1))) * mine + low for owner in owners]
    few_low = sum(side_of(bit) * (mine >> (k + 1)) for k, bit in enumerate(bits))
    end = at_end.astype(jnp.int32) if line else jnp.int32(0)
    base_at = 4 + len(bits)
    facts = [start, end, *map(side_of, bits), far_at, near_at, *bases, blk_at * mine + few_low]
    facts = jnp.stack(facts).astype(jnp.int32)

    def sum_rows(keep, got):
        for k, bit in enumerate(bits[1:]):
            keep, send = cut(3 + k, facts, keep, got)
            got = swap_red(send, bit)
        return keep, got

    def join_rows(value, which, *others):
        for k in reversed(which):
            got = after(swap_red(value, bits[k]), *others)
            value = join(2 + k, facts, value, got)
        return value

    head_at = blk_at // (blk_count // KV)
    one_head = lambda value: lax.dynamic_slice_in_dim(value, head_at * HD, HD, 1)
    cached = jnp.concatenate([one_head(cache_key), one_head(cache_value)], axis=1)

    token_at = (facts[base_at:-1, None] + jnp.arange(here, dtype=jnp.int32)).reshape(-1)
    few_at = facts[-1] + jnp.arange(few, dtype=jnp.int32)
    cosine, sine = tables(start + jnp.concatenate([token_at, few_at]))

    total_sq = jnp.sum(resid * resid, axis=1)
    for bit in bits:
        total_sq = total_sq + after(swap_red(total_sq, bit), facts)
    normed = (
        resid * lax.rsqrt(total_sq[:, None] / (width * red_count) + 1e-05) * norm_gain[None, :]
    ).astype(jnp.bfloat16)

    def pieces_of(value):
        return jnp.split(value, PIECES, axis=1)

    slots = range(far_count)
    last = far_count - 1
    hops = spread(normed)
    near = [swap_near(normed)]

    def ask(j, *others):
        return halves(facts, [after(far[j], *others), near[j]], [w_query])

    def have(*hops):
        return hops if line else ()

    def reduce(pair, got, *others):
        return sum_rows(after(pair[0], *others), got)

    def core(pair):
        return swap_red(pair[1], bits[0])

    half = mine // 2
    rest = range(1, len(bits))
    cached = after(cached, normed)[None]
    kv = halves(facts, [normed[:half], normed[half:]], [w_key, w_value])
    kv = reduce(kv, core(kv), near[0], hops[0], *have(hops[1]))
    cached = join_rows(cached, rest, kv[0])
    cached = cached.reshape(red_count // 2, -1, 2 * HD)
    shift = (blk_count // KV).bit_length() - 1
    same, other = pack(
        far_count * here, shift, base_at - 2, far_count, facts, *kv, cosine, sine
    )
    other = swap_near(other)
    far = [normed]
    asked = [ask(0, same, hops[0], *have(hops[1]))]
    moved = [core(asked[0])]
    keys, values = merge(facts, cached, after(swap_red(cached, bits[0]), asked[0][0]))
    fresh = jnp.stack([same, after(other, asked[0][0])], axis=1)
    held, bit = [fresh[d] for d in range(far_count)], 1

    def double(held, bit):
        send = jnp.concatenate(held[1::2])
        got = move_far(send, [(k, k ^ bit) for k in range(far_count)])
        return held[::2], got

    def settle(held, got):
        return [
            jnp.concatenate([one, part])
            for one, part in zip(held, jnp.split(got, len(held)))
        ]

    got = other
    while len(held) > 2:
        held, got = double(held, bit)
        held = settle(held, got)
        bit *= 2
    stage = got
    far += arrive(hops, facts, asked[0][0], stage)
    near += [swap_near(far[j]) for j in slots[1:]]
    held, got = double(held, bit)
    asked.append(ask(1, keys, far[2], stage, *have(hops[-1])))
    moved.append(core(asked[1]))
    fresh = settle(held, after(got, asked[1][0]))[0]
    asked[0] = reduce(asked[0], moved[0], asked[1][0])
    for j in range(2, last):
        asked.append(ask(j, asked[j - 2][0], far[j + 1], fresh))
        moved.append(core(asked[j]))
        if j < last - 1:
            asked[j - 1] = reduce(asked[j - 1], moved[j - 1], asked[j][0])
    rows = here * (w_query.shape[1] // HD)

    def mix(j, new, *others):
        keep, got = asked[j]
        old = [after(keep, *others), got, cosine, sine, keys, values]
        return attend(base_at, far_count, j, facts, here, rows, old, new)

    rest = range(1, len(bits))
    fresh = join_rows(fresh, rest, asked[last - 1][0])
    asked[last - 2] = reduce(asked[last - 2], moved[last - 2], fresh)
    begun = mix(0, None, asked[last - 2][0], fresh)
    fresh = join_rows(fresh, [0], begun[2]).reshape(blk_count * mine, 2 * HD)
    mixed = [None] * far_count
    mixed[0] = attend(base_at, far_count, 0, facts, here, rows, begun, fresh)
    asked.append(ask(last, mixed[0], asked[last - 2][1]))
    moved.append(core(asked[last]))

    parts = [None] * far_count
    per_half = red_count // 2
    turns = [
        sum(bit for i, bit in enumerate(bits[1:]) if k & (per_half >> (i + 1)))
        for k in range(per_half)
    ]
    turns = turns + [turn | bits[0] for turn in turns]

    def share(j):
        return [swap_red(mixed[j], turn) if turn else mixed[j] for turn in turns]

    def project(j, blocks, *others):
        blocks = [after(blocks[0], *others), *blocks[1:]]
        return halves(facts, blocks, [w_out])

    def finish(j, pair, *others):
        keep, send = pair
        send = after(send, *others)
        send = (send * SHRINK).astype(jnp.float16)
        send = [send] if j == 0 else pieces_of(send)
        got = [swap_near(p) for p in send]
        pieces = pieces_of(got[0]) if j == 0 else got
        parts[j] = [[p * SHRINK, g] for p, g in zip(pieces_of(keep), pieces)]
        return send, got

    shared = {0: share(0)}
    asked[last] = reduce(asked[last], moved[last])
    asked[last - 1] = reduce(asked[last - 1], moved[last - 1], asked[last][0])
    mixed[1] = mix(1, fresh, asked[last - 1][0])
    shared[1] = share(1)
    done, got = finish(0, project(0, shared[0], mixed[1], asked[last][1]))
    mixed[last] = mix(last, fresh, *done)
    shared[last] = share(last)
    done, got1 = finish(1, project(1, shared[1], mixed[last]))
    done = [*done, *got]
    for j in range(2, last):
        mixed[j] = mix(j, fresh, *done)
        shared[j] = share(j)
        done = [mixed[j]]
    first = [add(parts[1][0], *done)]
    hop = [(k, k ^ 1) for k in range(far_count)]
    passed = [move_far(first[0], hop)]
    done, _ = finish(last, project(last, shared[last], *done, first[0]))
    first.append(add(parts[1][1], *done, *(p for j in range(2, last) for p in shared[j][1:])))
    passed.append(move_far(first[1], hop))
    done = [*done, first[1]]
    for j in range(2, last):
        done, _ = finish(j, project(j, shared[j], *done))
    return resid + jnp.concatenate(collect(parts, passed, first[1]), axis=1) * (1.0 / SHRINK)


def solution(mesh):
    placed = (
        P("blk", "red"),
        P("red"),
        P("red", "blk"),
        P("red", None),
        P("red", None),
        P("blk", "red"),
        P("red", None),
        P("red", None),
        P(),
    )
    return jax.shard_map(
        on_device, mesh=mesh, in_specs=placed, out_specs=P("blk", "red"), check_vma=False
    )
```

```python
import functools
import math

import jax
import jax.numpy as jnp
from jax import lax
from jax.experimental import pallas as pl
from jax.experimental.pallas import tpu as pltpu
from jax.sharding import PartitionSpec as P

KV = 8
HD = 128
THETA = 500000.0
LOW = -1e30
RATE = HD**-0.5 / math.log(2.0)
SHRINK = 1.0 / 32.0
MIB = 1024 * 1024
PIECES = 2
COST = pl.CostEstimate(flops=0, bytes_accessed=0, transcendentals=0)


def tables(positions):
    half = HD // 2
    steps = jnp.arange(half, dtype=jnp.float32)
    freq = THETA ** (-(steps * 2.0) / HD)
    angle = positions.astype(jnp.float32)[..., None] * freq
    cosine, sine = jnp.cos(angle), jnp.sin(angle)
    return (
        jnp.concatenate([cosine, cosine], axis=-1),
        jnp.concatenate([-sine, sine], axis=-1),
    )


def fold(parts, peak, acc):
    lanes = [score[:, at : at + HD] for score, _ in parts for at in range(0, score.shape[1], HD)]
    top = jnp.max(functools.reduce(jnp.maximum, lanes), axis=1, keepdims=True)
    new_peak = jnp.maximum(peak, top)
    carry = jnp.exp2((peak - new_peak) * RATE)
    acc = acc * jnp.concatenate([carry, carry], axis=1)
    for score, values in parts:
        shift = jnp.concatenate([new_peak] * (score.shape[1] // HD), axis=1)
        weights = jnp.exp2((score - shift) * RATE).astype(jnp.bfloat16)
        both = jnp.concatenate([values, jnp.ones(values.shape, values.dtype)], axis=1)
        acc = acc + jnp.dot(weights, both, preferred_element_type=jnp.float32)
    return new_peak, acc


def scores(query, keys):
    return lax.dot_general(
        query, keys, (((1,), (1,)), ((), ())), preferred_element_type=jnp.float32
    )


def attention_kernel(base_at, far_count, slot, unit, tile, cached, spanned, *refs):
    refs = list(refs)
    facts_ref = refs.pop(0)
    if cached:
        keep_ref, got_ref, cos_ref, sin_ref, key_ref, value_ref = refs[:6]
        refs = refs[6:]
    else:
        old_q_ref, old_peak_ref, old_acc_ref = refs[:3]
        refs = refs[3:]
    if spanned:
        fresh_ref, out_ref = refs[:2]
        refs = refs[2:]
    q_ref, peak_ref, acc_ref = refs if cached else (old_q_ref, old_peak_ref, old_acc_ref)
    start = facts_ref[0]
    rows_here = q_ref.shape[0]
    tiles = [slice(low, low + tile) for low in range(0, rows_here, tile)]

    def step(base, count, masked):
        for rows in tiles:
            parts = []
            for k in range(count):
                low = pl.multiple_of(base + k * unit, unit)
                here = pl.ds(low, unit)
                score = jnp.dot(
                    q_ref[rows, :], key_ref[:, here], preferred_element_type=jnp.float32
                )
                if masked and k == count - 1:
                    at = low + lax.broadcasted_iota(jnp.int32, (1, unit), 1)
                    score = jnp.where(at < start, score, LOW)
                parts.append((score, value_ref[here, :]))
            peak_ref[rows, :], acc_ref[rows, :] = fold(parts, peak_ref[rows, :], acc_ref[rows, :])

    if cached:
        tokens = keep_ref.shape[0]
        mine = slice(slot * tokens, (slot + 1) * tokens)
        cosine, sine = cos_ref[mine, :], sin_ref[mine, :]
        rotated = []
        for head in range(keep_ref.shape[1] // HD):
            at = slice(head * HD, (head + 1) * HD)
            raw = keep_ref[:, at] + got_ref[:, at]
            rotated.append(raw * cosine + pltpu.roll(raw, HD // 2, 1) * sine)
        q_ref[...] = jnp.concatenate(rotated, axis=0).astype(q_ref.dtype)
        peak_ref[...] = jnp.full(peak_ref.shape, LOW, jnp.float32)
        acc_ref[...] = jnp.zeros(acc_ref.shape, jnp.float32)
        pairs = start // (2 * unit)
        done = pairs * (2 * unit)

        @pl.loop(0, pairs)
        def _(index):
            step(index * (2 * unit), 2, False)

        @pl.when((start > done) & (start <= done + unit))
        def _():
            step(done, 1, True)

        @pl.when(start > done + unit)
        def _():
            step(done, 2, True)

    if spanned:
        tokens = out_ref.shape[0]
        keys, values = fresh_ref[:, :HD], fresh_ref[:, HD:]
        far, near = facts_ref[base_at - 2], facts_ref[base_at - 1]
        own = fresh_ref.shape[0] // (2 * far_count)
        in_block = lax.broadcasted_iota(jnp.int32, (1, own), 1)
        key_at = jnp.concatenate(
            [
                in_block + ((far ^ d) * 2 + (near ^ k)) * own
                for d in range(far_count)
                for k in range(2)
            ],
            axis=1,
        )
        query_at = facts_ref[base_at + slot] + lax.broadcasted_iota(jnp.int32, (tokens, 1), 0)
        query_at = jnp.concatenate([query_at] * (tile // tokens), axis=0)
        for rows in tiles:
            score = jnp.where(key_at <= query_at, scores(q_ref[rows, :], keys), LOW)
            _, acc = fold([(score, values)], peak_ref[rows, :], acc_ref[rows, :])
            mixed = (acc[:, :HD] / acc[:, HD:]).astype(out_ref.dtype)
            for part in range(tile // tokens):
                head = rows.start // tokens + part
                out_ref[:, head * HD : (head + 1) * HD] = mixed[
                    part * tokens : (part + 1) * tokens
                ]


def attend(base_at, far_count, slot, facts, tokens, rows, old, new):
    cached = len(old) == 6
    spanned = new is not None
    unit = min(1024, old[5].shape[0] // 2) if cached else 0
    tile = min(256, rows)
    vmem = pl.BlockSpec(memory_space=pltpu.VMEM)
    state = [
        ((rows, HD), jnp.bfloat16),
        ((rows, HD), jnp.float32),
        ((rows, 2 * HD), jnp.float32),
    ]
    if spanned:
        out_shape = jax.ShapeDtypeStruct((tokens, rows // tokens * HD), jnp.bfloat16)
    else:
        out_shape = tuple(jax.ShapeDtypeStruct(*one) for one in state)
    operands = [*old, *([new] if spanned else [])]
    return pl.pallas_call(
        functools.partial(attention_kernel, base_at, far_count, slot, unit, tile, cached, spanned),
        out_shape=out_shape,
        in_specs=[pl.BlockSpec(memory_space=pltpu.SMEM)] + [vmem] * len(operands),
        out_specs=vmem if spanned else (vmem,) * 3,
        scratch_shapes=[pltpu.VMEM(*one) for one in state] if cached and spanned else [],
        compiler_params=pltpu.CompilerParams(vmem_limit_bytes=(9 if cached else 5) * MIB),
        cost_estimate=pl.CostEstimate(
            flops=8 * rows * HD * (old[5].shape[0] + new.shape[0]) if cached and spanned else 0,
            bytes_accessed=0,
            transcendentals=0,
        ),
        name="attention",
    )(facts, *operands)


def small_call(kernel, name, out_shape, facts, *operands):
    vmem = pl.BlockSpec(memory_space=pltpu.VMEM)
    return pl.pallas_call(
        kernel,
        out_shape=out_shape,
        in_specs=[pl.BlockSpec(memory_space=pltpu.SMEM)] + [vmem] * len(operands),
        out_specs=jax.tree.map(lambda _: vmem, out_shape),
        compiler_params=pltpu.CompilerParams(vmem_limit_bytes=4 * MIB),
        cost_estimate=COST,
        name=name,
    )(facts, *operands)


def cut_kernel(fact, facts_ref, keep_ref, got_ref, mine_ref, send_ref):
    half = mine_ref.shape[0]
    upper = facts_ref[fact] == 1
    low, high = (keep_ref[at, :] + got_ref[at, :] for at in (slice(0, half), slice(half, None)))
    mine_ref[...] = jnp.where(upper, high, low)
    send_ref[...] = jnp.where(upper, low, high)


def cut(fact, facts, keep, got):
    out = jax.ShapeDtypeStruct((keep.shape[0] // 2, keep.shape[1]), keep.dtype)
    return small_call(functools.partial(cut_kernel, fact), "cut", (out, out), facts, keep, got)


def join_kernel(fact, facts_ref, own_ref, got_ref, out_ref):
    half = own_ref.shape[1]
    upper = facts_ref[fact] == 1

    @pl.when(upper)
    def _():
        out_ref[:, :half] = got_ref[...]
        out_ref[:, half:] = own_ref[...]

    @pl.when(jnp.logical_not(upper))
    def _():
        out_ref[:, :half] = own_ref[...]
        out_ref[:, half:] = got_ref[...]


def join(fact, facts, own, got):
    count, half, width = own.shape
    if half % 16:
        upper = facts[fact] == 1
        return jnp.where(
            upper, jnp.concatenate([got, own], axis=1), jnp.concatenate([own, got], axis=1)
        )
    out = jax.ShapeDtypeStruct((count, 2 * half, width), own.dtype)
    return small_call(functools.partial(join_kernel, fact), "join", out, facts, own, got)


def merge_kernel(facts_ref, own_ref, got_ref, key_ref, value_ref):
    count, rows, _ = own_ref.shape
    for side in range(2):

        @pl.when(facts_ref[2] == side)
        def _():
            for k in range(count):
                for at, ref in ((2 * k + side, own_ref), (2 * k + 1 - side, got_ref)):
                    here = slice(at * rows, (at + 1) * rows)
                    key_ref[:, here] = ref[k, :, :HD].astype(jnp.float32).T.astype(key_ref.dtype)
                    value_ref[here, :] = ref[k, :, HD:]


def merge(facts, own, got):
    slots = 2 * own.shape[0] * own.shape[1]
    out = (
        jax.ShapeDtypeStruct((HD, slots), own.dtype),
        jax.ShapeDtypeStruct((slots, HD), own.dtype),
    )
    return small_call(merge_kernel, "merge", out, facts, own, got)


def pick_kernel(facts_ref, a_ref, b_ref, out_ref):
    @pl.when(facts_ref[1] == 1)
    def _():
        out_ref[...] = a_ref[...]

    @pl.when(facts_ref[1] != 1)
    def _():
        out_ref[...] = b_ref[...]


def pick(facts, a, b):
    return small_call(pick_kernel, "pick", jax.ShapeDtypeStruct(a.shape, a.dtype), facts, a, b)


def halves_kernel(blocks, tile, facts_ref, *refs):
    lhs, refs = refs[:blocks], refs[blocks:]
    w_refs, (keep_ref, send_ref) = refs[:-2], refs[-2:]
    rows, per_half = lhs[0].shape[0], blocks // 2
    upper, place = facts_ref[2] == 1, facts_ref[2] * 0
    for k in range(per_half.bit_length() - 1):
        place = place + facts_ref[3 + k] * (per_half >> (k + 1))
    both = jnp.concatenate([ref[...] for ref in lhs], axis=0)
    low = 0
    for w_ref in w_refs:

        @pl.loop(0, w_ref.shape[1] // tile)
        def _(step, low=low, w_ref=w_ref):
            at = pl.multiple_of(step * tile, tile)
            out = jnp.dot(both, w_ref[:, pl.ds(at, tile)], preferred_element_type=jnp.float32)
            here = pl.ds(pl.multiple_of(low + at, tile), tile)
            half = per_half * rows
            first = jnp.where(upper, out[half:], out[:half])
            second = jnp.where(upper, out[:half], out[half:])
            for k in range(per_half):
                to = pl.ds(pl.multiple_of((place ^ k) * rows, rows), rows)
                keep_ref[to, here] = first[k * rows : (k + 1) * rows]
                send_ref[to, here] = second[k * rows : (k + 1) * rows]

        low += w_ref.shape[1]


def halves(facts, lhs, weights):
    rows = lhs[0].shape[0] * len(lhs) // 2
    width = sum(w.shape[1] for w in weights)
    out = jax.ShapeDtypeStruct((rows, width), jnp.float32)
    vmem = pl.BlockSpec(memory_space=pltpu.VMEM)
    operands = [*lhs, *weights]
    return pl.pallas_call(
        functools.partial(halves_kernel, len(lhs), min(512, weights[0].shape[1])),
        out_shape=(out, out),
        in_specs=[pl.BlockSpec(memory_space=pltpu.SMEM)] + [vmem] * len(operands),
        out_specs=(vmem, vmem),
        compiler_params=pltpu.CompilerParams(vmem_limit_bytes=5 * MIB),
        cost_estimate=pl.CostEstimate(
            flops=4 * rows * weights[0].shape[0] * width, bytes_accessed=0, transcendentals=0
        ),
        name="halves",
    )(facts, *operands)


def pack_kernel(low, shift, where_at, facts_ref, keep_ref, got_ref, cos_ref, sin_ref, same_ref, other_ref):
    few = keep_ref.shape[0]
    cosine, sine = cos_ref[low : low + few, :], sin_ref[low : low + few, :]
    far, near = facts_ref[where_at], facts_ref[where_at + 1]
    for d in range(same_ref.shape[0]):
        for k, out_ref in enumerate((same_ref, other_ref)):
            head = ((far ^ d) * 2 + (near ^ k)) >> shift
            raw, value = (
                keep_ref[:, pl.ds(pl.multiple_of(at * HD, HD), HD)]
                + got_ref[:, pl.ds(pl.multiple_of(at * HD, HD), HD)]
                for at in (head, KV + head)
            )
            both = [raw * cosine + pltpu.roll(raw, HD // 2, 1) * sine, value]
            out_ref[d] = jnp.concatenate(both, axis=1).astype(out_ref.dtype)


def pack(low, shift, where_at, count, facts, keep, got, cosine, sine):
    out = jax.ShapeDtypeStruct((count, keep.shape[0], 2 * HD), jnp.bfloat16)
    kernel = functools.partial(pack_kernel, low, shift, where_at)
    return small_call(kernel, "pack", (out, out), facts, keep, got, cosine, sine)


def on_device(resid, norm_gain, w_query, w_key, w_value, w_out, cache_key, cache_value, prefix_len):
    blk_count, red_count = lax.axis_size("blk"), lax.axis_size("red")
    blk_at, red_at = lax.axis_index("blk"), lax.axis_index("red")
    start = prefix_len[0]
    mine, width = resid.shape
    far_count = blk_count // 2
    far_at, near_at = blk_at // 2, blk_at % 2
    bits = [1 << k for k in range(red_count.bit_length() - 1)]

    def swap_red(value, bit):
        return lax.ppermute(value, "red", [(k, k ^ bit) for k in range(red_count)])

    def swap_near(value):
        return lax.ppermute(value, "blk", [(k, k ^ 1) for k in range(blk_count)])

    def move_far(value, pairs):
        pairs = [(2 * a + k, 2 * b + k) for a, b in pairs for k in range(2)]
        return lax.ppermute(value, "blk", pairs)

    line = far_count == 4
    if line:
        at_end = (far_at == 0) | (far_at == 3)
        pairs_out = [(1, 0), (2, 3)]
        pairs_in = [(0, 1), (3, 2)]
        middle = [(1, 2), (2, 1)]
        owners = [
            far_at,
            far_at ^ 1,
            far_at ^ jnp.where(at_end, 2, 3),
            far_at ^ jnp.where(at_end, 3, 2),
        ]
    else:
        owners = [(far_at + j) % far_count for j in range(far_count)]

    def spread(own):
        if not line:
            ring = range(far_count)
            return [move_far(own, [((k + j) % far_count, k) for k in ring]) for j in ring if j > 0]
        a1 = move_far(own, pairs_out + pairs_in)
        b1 = move_far(own, middle)
        return [a1, b1, move_far(b1, pairs_out), move_far(a1, middle)]

    def arrive(hops, facts, *others):
        if not line:
            return hops
        a1, b1, a2, b2 = hops
        a3 = move_far(after(b2, *others), pairs_out)
        return [a1, pick(facts, a2, b1), (a3, b2)]

    wide = lambda value: value.astype(jnp.float32)

    def add(terms, *others):
        return sum(map(wide, [*terms[:-1], after(terms[-1], *others)])).astype(jnp.float16)

    def collect(parts, passed, first):
        own = [list(terms) for terms in parts[0]]
        if line:
            s2, s3 = parts[2:]
            last = first
            stages = {}

            def go(name, terms, pairs, *others):
                nonlocal last
                last = add(terms, last, *others)
                stages[name] = move_far(last, pairs)

            go("a3", s3[0], pairs_in)
            go("a3+", s3[1], pairs_in)
            go("b2", s3[0] + [stages["a3"]], middle, passed[0])
            go("a2", s2[0], pairs_in)
            go("b2+", s3[1] + [stages["a3+"]], middle, passed[1])
            go("c1", [stages["b2"]], pairs_out)
            go("a2+", s2[1], pairs_in)
            go("b1", s2[0] + [stages["a2"]], middle)
            go("c1+", [stages["b2+"]], pairs_out)
            go("b1+", s2[1] + [stages["a2+"]], middle)
            for k, end in enumerate(("", "+")):
                own[k] += [passed[k], stages["c1" + end], stages["b1" + end]]
        else:
            ring = range(far_count)
            for j in ring:
                for k, terms in enumerate(parts[j] if j > 0 else []):
                    own[k].append(
                        move_far(add(terms), [(i, (i + j) % far_count) for i in ring])
                    )
        return [sum(map(wide, terms)) for terms in own]

    def after(value, *others):
        return lax.optimization_barrier((value, *others))[0] if others else value

    def side_of(bit):
        return (red_at // bit) % 2

    here, few = 2 * mine // red_count, mine // red_count
    low = sum(side_of(bit) * (mine >> k) for k, bit in enumerate(bits) if k > 0)
    bases = [(owner * 2 + (near_at ^ side_of(1))) * mine + low for owner in owners]
    few_low = sum(side_of(bit) * (mine >> (k + 1)) for k, bit in enumerate(bits))
    end = at_end.astype(jnp.int32) if line else jnp.int32(0)
    base_at = 4 + len(bits)
    facts = [start, end, *map(side_of, bits), far_at, near_at, *bases, blk_at * mine + few_low]
    facts = jnp.stack(facts).astype(jnp.int32)

    def sum_rows(keep, got):
        for k, bit in enumerate(bits[1:]):
            keep, send = cut(3 + k, facts, keep, got)
            got = swap_red(send, bit)
        return keep, got

    def join_rows(value, which, *others):
        for k in reversed(which):
            got = after(swap_red(value, bits[k]), *others)
            value = join(2 + k, facts, value, got)
        return value

    head_at = blk_at // (blk_count // KV)
    one_head = lambda value: lax.dynamic_slice_in_dim(value, head_at * HD, HD, 1)
    cached = jnp.concatenate([one_head(cache_key), one_head(cache_value)], axis=1)

    token_at = (facts[base_at:-1, None] + jnp.arange(here, dtype=jnp.int32)).reshape(-1)
    few_at = facts[-1] + jnp.arange(few, dtype=jnp.int32)
    cosine, sine = tables(start + jnp.concatenate([token_at, few_at]))

    total_sq = jnp.sum(resid * resid, axis=1)
    for bit in bits:
        total_sq = total_sq + after(swap_red(total_sq, bit), facts)
    normed = (
        resid * lax.rsqrt(total_sq[:, None] / (width * red_count) + 1e-05) * norm_gain[None, :]
    ).astype(jnp.bfloat16)

    def pieces_of(value):
        return jnp.split(value, PIECES, axis=1)

    slots = range(far_count)
    last = far_count - 1
    hops = spread(normed)
    near = [swap_near(normed)]

    def ask(j, *others):
        return halves(facts, [after(far[j], *others), near[j]], [w_query])

    def have(*hops):
        return hops if line else ()

    def reduce(pair, got, *others):
        return sum_rows(after(pair[0], *others), got)

    def core(pair):
        return swap_red(pair[1], bits[0])

    half = mine // 2
    rest = range(1, len(bits))
    cached = after(cached, normed)[None]
    kv = halves(facts, [normed[:half], normed[half:]], [w_key, w_value])
    kv = reduce(kv, core(kv), near[0], hops[0], *have(hops[1]))
    cached = join_rows(cached, rest, kv[0])
    cached = cached.reshape(red_count // 2, -1, 2 * HD)
    shift = (blk_count // KV).bit_length() - 1
    same, other = pack(
        far_count * here, shift, base_at - 2, far_count, facts, *kv, cosine, sine
    )
    other = swap_near(other)
    far = [normed]
    asked = [ask(0, same, hops[0], *have(hops[1]))]
    moved = [core(asked[0])]
    keys, values = merge(facts, cached, after(swap_red(cached, bits[0]), asked[0][0]))
    fresh = jnp.stack([same, after(other, asked[0][0])], axis=1)
    held, bit = [fresh[d] for d in range(far_count)], 1

    def double(held, bit):
        send = jnp.concatenate(held[1::2])
        got = move_far(send, [(k, k ^ bit) for k in range(far_count)])
        return held[::2], got

    def settle(held, got):
        return [
            jnp.concatenate([one, part])
            for one, part in zip(held, jnp.split(got, len(held)))
        ]

    got = other
    while len(held) > 2:
        held, got = double(held, bit)
        held = settle(held, got)
        bit *= 2
    stage = got
    far += arrive(hops, facts, asked[0][0], stage)
    near += [swap_near(far[j]) for j in slots[1 : last if line else None]]
    held, got = double(held, bit)
    asked.append(ask(1, keys, far[2], stage, *have(hops[-1])))
    moved.append(core(asked[1]))
    fresh = settle(held, after(got, asked[1][0]))[0]
    asked[0] = reduce(asked[0], moved[0], asked[1][0])
    if line:
        a3, b2 = far[last]
        far[last] = pick(facts, after(a3, asked[0][0]), b2)
        near.append(swap_near(far[last]))
    for j in range(2, last):
        asked.append(ask(j, asked[j - 2][0], far[j + 1], fresh))
        moved.append(core(asked[j]))
        if j < last - 1:
            asked[j - 1] = reduce(asked[j - 1], moved[j - 1], asked[j][0])
    rows = here * (w_query.shape[1] // HD)

    def mix(j, new, *others):
        keep, got = asked[j]
        old = [after(keep, *others), got, cosine, sine, keys, values]
        return attend(base_at, far_count, j, facts, here, rows, old, new)

    rest = range(1, len(bits))
    fresh = join_rows(fresh, rest, asked[last - 1][0])
    asked[last - 2] = reduce(asked[last - 2], moved[last - 2], fresh)
    begun = mix(0, None, asked[last - 2][0], fresh)
    fresh = join_rows(fresh, [0], begun[2]).reshape(blk_count * mine, 2 * HD)
    mixed = [None] * far_count
    mixed[0] = attend(base_at, far_count, 0, facts, here, rows, begun, fresh)
    asked.append(ask(last, mixed[0], asked[last - 2][1]))
    moved.append(core(asked[last]))

    parts = [None] * far_count
    per_half = red_count // 2
    turns = [
        sum(bit for i, bit in enumerate(bits[1:]) if k & (per_half >> (i + 1)))
        for k in range(per_half)
    ]
    turns = turns + [turn | bits[0] for turn in turns]

    def share(j):
        return [swap_red(mixed[j], turn) if turn else mixed[j] for turn in turns]

    def project(j, blocks, *others):
        blocks = [after(blocks[0], *others), *blocks[1:]]
        return halves(facts, blocks, [w_out])

    def finish(j, pair, *others):
        keep, send = pair
        send = after(send, *others)
        send = (send * SHRINK).astype(jnp.float16)
        send = [send] if j == 0 else pieces_of(send)
        got = [swap_near(p) for p in send]
        pieces = pieces_of(got[0]) if j == 0 else got
        parts[j] = [[p * SHRINK, g] for p, g in zip(pieces_of(keep), pieces)]
        return send, got

    asked[last] = reduce(asked[last], moved[last])
    asked[last - 1] = reduce(asked[last - 1], moved[last - 1], asked[last][0])
    mixed[1] = mix(1, fresh, asked[last - 1][0])
    shared = {1: share(1)}
    done, got1 = finish(1, project(1, shared[1], mixed[1], asked[last][1]))
    mixed[0] = after(mixed[0], *done)
    shared[0] = share(0)
    mixed[last] = mix(last, fresh, *done)
    shared[last] = share(last)
    first = [add(parts[1][0], mixed[last])]
    hop = [(k, k ^ 1) for k in range(far_count)]
    passed = [move_far(first[0], hop)]
    done = [mixed[last], first[0]]
    for j in range(2, last):
        mixed[j] = mix(j, fresh, *done)
        shared[j] = share(j)
        done = [mixed[j]]
    first.append(add(parts[1][1], *done))
    passed.append(move_far(first[1], hop))
    done, _ = finish(last, project(last, shared[last], *done, first[1], passed[0]))
    late = project(0, shared[0], *done)
    done = [late[0], passed[1]]
    for j in range(2, last):
        done, _ = finish(j, project(j, shared[j], *done))
    finish(0, late, *done)
    return resid + jnp.concatenate(collect(parts, passed, first[1]), axis=1) * (1.0 / SHRINK)


def solution(mesh):
    placed = (
        P("blk", "red"),
        P("red"),
        P("red", "blk"),
        P("red", None),
        P("red", None),
        P("blk", "red"),
        P("red", None),
        P("red", None),
        P(),
    )
    return jax.shard_map(
        on_device, mesh=mesh, in_specs=placed, out_specs=P("blk", "red"), check_vma=False
    )
```

```python
import functools
import math

import jax
import jax.numpy as jnp
from jax import lax
from jax.experimental import pallas as pl
from jax.experimental.pallas import tpu as pltpu
from jax.sharding import PartitionSpec as P

KV = 8
HD = 128
THETA = 500000.0
LOW = -1e30
RATE = HD**-0.5 / math.log(2.0)
SHRINK = 1.0 / 32.0
MIB = 1024 * 1024
PIECES = 2
COST = pl.CostEstimate(flops=0, bytes_accessed=0, transcendentals=0)


def tables(positions):
    half = HD // 2
    steps = jnp.arange(half, dtype=jnp.float32)
    freq = THETA ** (-(steps * 2.0) / HD)
    angle = positions.astype(jnp.float32)[..., None] * freq
    cosine, sine = jnp.cos(angle), jnp.sin(angle)
    return (
        jnp.concatenate([cosine, cosine], axis=-1),
        jnp.concatenate([-sine, sine], axis=-1),
    )


def fold(parts, peak, acc):
    lanes = [score[:, at : at + HD] for score, _ in parts for at in range(0, score.shape[1], HD)]
    top = jnp.max(functools.reduce(jnp.maximum, lanes), axis=1, keepdims=True)
    new_peak = jnp.maximum(peak, top)
    carry = jnp.exp2((peak - new_peak) * RATE)
    acc = acc * jnp.concatenate([carry, carry], axis=1)
    for score, values in parts:
        shift = jnp.concatenate([new_peak] * (score.shape[1] // HD), axis=1)
        weights = jnp.exp2((score - shift) * RATE).astype(jnp.bfloat16)
        both = jnp.concatenate([values, jnp.ones(values.shape, values.dtype)], axis=1)
        acc = acc + jnp.dot(weights, both, preferred_element_type=jnp.float32)
    return new_peak, acc


def scores(query, keys):
    return lax.dot_general(
        query, keys, (((1,), (1,)), ((), ())), preferred_element_type=jnp.float32
    )


def attention_kernel(base_at, far_count, slot, unit, tile, cached, spanned, *refs):
    refs = list(refs)
    facts_ref = refs.pop(0)
    if cached:
        keep_ref, got_ref, cos_ref, sin_ref, key_ref, value_ref = refs[:6]
        refs = refs[6:]
    else:
        old_q_ref, old_peak_ref, old_acc_ref = refs[:3]
        refs = refs[3:]
    if spanned:
        fresh_ref, out_ref = refs[:2]
        refs = refs[2:]
    q_ref, peak_ref, acc_ref = refs if cached else (old_q_ref, old_peak_ref, old_acc_ref)
    start = facts_ref[0]
    rows_here = q_ref.shape[0]
    tiles = [slice(low, low + tile) for low in range(0, rows_here, tile)]

    def step(base, count, masked):
        for rows in tiles:
            parts = []
            for k in range(count):
                low = pl.multiple_of(base + k * unit, unit)
                here = pl.ds(low, unit)
                score = jnp.dot(
                    q_ref[rows, :], key_ref[:, here], preferred_element_type=jnp.float32
                )
                if masked and k == count - 1:
                    at = low + lax.broadcasted_iota(jnp.int32, (1, unit), 1)
                    score = jnp.where(at < start, score, LOW)
                parts.append((score, value_ref[here, :]))
            peak_ref[rows, :], acc_ref[rows, :] = fold(parts, peak_ref[rows, :], acc_ref[rows, :])

    if cached:
        tokens = keep_ref.shape[0]
        mine = slice(slot * tokens, (slot + 1) * tokens)
        cosine, sine = cos_ref[mine, :], sin_ref[mine, :]
        rotated = []
        for head in range(keep_ref.shape[1] // HD):
            at = slice(head * HD, (head + 1) * HD)
            raw = keep_ref[:, at] + got_ref[:, at]
            rotated.append(raw * cosine + pltpu.roll(raw, HD // 2, 1) * sine)
        q_ref[...] = jnp.concatenate(rotated, axis=0).astype(q_ref.dtype)
        peak_ref[...] = jnp.full(peak_ref.shape, LOW, jnp.float32)
        acc_ref[...] = jnp.zeros(acc_ref.shape, jnp.float32)
        pairs = start // (2 * unit)
        done = pairs * (2 * unit)

        @pl.loop(0, pairs)
        def _(index):
            step(index * (2 * unit), 2, False)

        @pl.when((start > done) & (start <= done + unit))
        def _():
            step(done, 1, True)

        @pl.when(start > done + unit)
        def _():
            step(done, 2, True)

    if spanned:
        tokens = out_ref.shape[0]
        keys, values = fresh_ref[:, :HD], fresh_ref[:, HD:]
        far, near = facts_ref[base_at - 2], facts_ref[base_at - 1]
        own = fresh_ref.shape[0] // (2 * far_count)
        in_block = lax.broadcasted_iota(jnp.int32, (1, own), 1)
        key_at = jnp.concatenate(
            [
                in_block + ((far ^ d) * 2 + (near ^ k)) * own
                for d in range(far_count)
                for k in range(2)
            ],
            axis=1,
        )
        query_at = facts_ref[base_at + slot] + lax.broadcasted_iota(jnp.int32, (tokens, 1), 0)
        query_at = jnp.concatenate([query_at] * (tile // tokens), axis=0)
        for rows in tiles:
            score = jnp.where(key_at <= query_at, scores(q_ref[rows, :], keys), LOW)
            _, acc = fold([(score, values)], peak_ref[rows, :], acc_ref[rows, :])
            mixed = (acc[:, :HD] / acc[:, HD:]).astype(out_ref.dtype)
            for part in range(tile // tokens):
                head = rows.start // tokens + part
                out_ref[:, head * HD : (head + 1) * HD] = mixed[
                    part * tokens : (part + 1) * tokens
                ]


def attend(base_at, far_count, slot, facts, tokens, rows, old, new):
    cached = len(old) == 6
    spanned = new is not None
    unit = min(1024, old[5].shape[0] // 2) if cached else 0
    tile = min(256, rows)
    vmem = pl.BlockSpec(memory_space=pltpu.VMEM)
    state = [
        ((rows, HD), jnp.bfloat16),
        ((rows, HD), jnp.float32),
        ((rows, 2 * HD), jnp.float32),
    ]
    if spanned:
        out_shape = jax.ShapeDtypeStruct((tokens, rows // tokens * HD), jnp.bfloat16)
    else:
        out_shape = tuple(jax.ShapeDtypeStruct(*one) for one in state)
    operands = [*old, *([new] if spanned else [])]
    return pl.pallas_call(
        functools.partial(attention_kernel, base_at, far_count, slot, unit, tile, cached, spanned),
        out_shape=out_shape,
        in_specs=[pl.BlockSpec(memory_space=pltpu.SMEM)] + [vmem] * len(operands),
        out_specs=vmem if spanned else (vmem,) * 3,
        scratch_shapes=[pltpu.VMEM(*one) for one in state] if cached and spanned else [],
        compiler_params=pltpu.CompilerParams(vmem_limit_bytes=(9 if cached else 5) * MIB),
        cost_estimate=pl.CostEstimate(
            flops=8 * rows * HD * (old[5].shape[0] + new.shape[0]) if cached and spanned else 0,
            bytes_accessed=0,
            transcendentals=0,
        ),
        name="attention",
    )(facts, *operands)


def small_call(kernel, name, out_shape, facts, *operands):
    vmem = pl.BlockSpec(memory_space=pltpu.VMEM)
    return pl.pallas_call(
        kernel,
        out_shape=out_shape,
        in_specs=[pl.BlockSpec(memory_space=pltpu.SMEM)] + [vmem] * len(operands),
        out_specs=jax.tree.map(lambda _: vmem, out_shape),
        compiler_params=pltpu.CompilerParams(vmem_limit_bytes=4 * MIB),
        cost_estimate=COST,
        name=name,
    )(facts, *operands)


def cut_kernel(fact, facts_ref, keep_ref, got_ref, mine_ref, send_ref):
    half = mine_ref.shape[0]
    upper = facts_ref[fact] == 1
    low, high = (keep_ref[at, :] + got_ref[at, :] for at in (slice(0, half), slice(half, None)))
    mine_ref[...] = jnp.where(upper, high, low)
    send_ref[...] = jnp.where(upper, low, high)


def cut(fact, facts, keep, got):
    out = jax.ShapeDtypeStruct((keep.shape[0] // 2, keep.shape[1]), keep.dtype)
    return small_call(functools.partial(cut_kernel, fact), "cut", (out, out), facts, keep, got)


def join_kernel(fact, facts_ref, own_ref, got_ref, out_ref):
    half = own_ref.shape[1]
    upper = facts_ref[fact] == 1

    @pl.when(upper)
    def _():
        out_ref[:, :half] = got_ref[...]
        out_ref[:, half:] = own_ref[...]

    @pl.when(jnp.logical_not(upper))
    def _():
        out_ref[:, :half] = own_ref[...]
        out_ref[:, half:] = got_ref[...]


def join(fact, facts, own, got):
    count, half, width = own.shape
    if half % 16:
        upper = facts[fact] == 1
        return jnp.where(
            upper, jnp.concatenate([got, own], axis=1), jnp.concatenate([own, got], axis=1)
        )
    out = jax.ShapeDtypeStruct((count, 2 * half, width), own.dtype)
    return small_call(functools.partial(join_kernel, fact), "join", out, facts, own, got)


def merge_kernel(facts_ref, own_ref, got_ref, key_ref, value_ref):
    count, rows, _ = own_ref.shape
    for side in range(2):

        @pl.when(facts_ref[2] == side)
        def _():
            for k in range(count):
                for at, ref in ((2 * k + side, own_ref), (2 * k + 1 - side, got_ref)):
                    here = slice(at * rows, (at + 1) * rows)
                    key_ref[:, here] = ref[k, :, :HD].astype(jnp.float32).T.astype(key_ref.dtype)
                    value_ref[here, :] = ref[k, :, HD:]


def merge(facts, own, got):
    slots = 2 * own.shape[0] * own.shape[1]
    out = (
        jax.ShapeDtypeStruct((HD, slots), own.dtype),
        jax.ShapeDtypeStruct((slots, HD), own.dtype),
    )
    return small_call(merge_kernel, "merge", out, facts, own, got)


def pick_kernel(facts_ref, a_ref, b_ref, out_ref):
    @pl.when(facts_ref[1] == 1)
    def _():
        out_ref[...] = a_ref[...]

    @pl.when(facts_ref[1] != 1)
    def _():
        out_ref[...] = b_ref[...]


def pick(facts, a, b):
    return small_call(pick_kernel, "pick", jax.ShapeDtypeStruct(a.shape, a.dtype), facts, a, b)


def halves_kernel(blocks, tile, facts_ref, *refs):
    lhs, refs = refs[:blocks], refs[blocks:]
    w_refs, (keep_ref, send_ref) = refs[:-2], refs[-2:]
    rows, per_half = lhs[0].shape[0], blocks // 2
    upper, place = facts_ref[2] == 1, facts_ref[2] * 0
    for k in range(per_half.bit_length() - 1):
        place = place + facts_ref[3 + k] * (per_half >> (k + 1))
    both = jnp.concatenate([ref[...] for ref in lhs], axis=0)
    low = 0
    for w_ref in w_refs:

        @pl.loop(0, w_ref.shape[1] // tile)
        def _(step, low=low, w_ref=w_ref):
            at = pl.multiple_of(step * tile, tile)
            out = jnp.dot(both, w_ref[:, pl.ds(at, tile)], preferred_element_type=jnp.float32)
            here = pl.ds(pl.multiple_of(low + at, tile), tile)
            half = per_half * rows
            first = jnp.where(upper, out[half:], out[:half])
            second = jnp.where(upper, out[:half], out[half:])
            for k in range(per_half):
                to = pl.ds(pl.multiple_of((place ^ k) * rows, rows), rows)
                keep_ref[to, here] = first[k * rows : (k + 1) * rows]
                send_ref[to, here] = second[k * rows : (k + 1) * rows]

        low += w_ref.shape[1]


def halves(facts, lhs, weights):
    rows = lhs[0].shape[0] * len(lhs) // 2
    width = sum(w.shape[1] for w in weights)
    out = jax.ShapeDtypeStruct((rows, width), jnp.float32)
    vmem = pl.BlockSpec(memory_space=pltpu.VMEM)
    operands = [*lhs, *weights]
    return pl.pallas_call(
        functools.partial(halves_kernel, len(lhs), min(512, weights[0].shape[1])),
        out_shape=(out, out),
        in_specs=[pl.BlockSpec(memory_space=pltpu.SMEM)] + [vmem] * len(operands),
        out_specs=(vmem, vmem),
        compiler_params=pltpu.CompilerParams(vmem_limit_bytes=5 * MIB),
        cost_estimate=pl.CostEstimate(
            flops=4 * rows * weights[0].shape[0] * width, bytes_accessed=0, transcendentals=0
        ),
        name="halves",
    )(facts, *operands)


def pack_kernel(low, shift, where_at, facts_ref, keep_ref, got_ref, cos_ref, sin_ref, same_ref, other_ref):
    few = keep_ref.shape[0]
    cosine, sine = cos_ref[low : low + few, :], sin_ref[low : low + few, :]
    far, near = facts_ref[where_at], facts_ref[where_at + 1]
    for d in range(same_ref.shape[0]):
        for k, out_ref in enumerate((same_ref, other_ref)):
            head = ((far ^ d) * 2 + (near ^ k)) >> shift
            raw, value = (
                keep_ref[:, pl.ds(pl.multiple_of(at * HD, HD), HD)]
                + got_ref[:, pl.ds(pl.multiple_of(at * HD, HD), HD)]
                for at in (head, KV + head)
            )
            both = [raw * cosine + pltpu.roll(raw, HD // 2, 1) * sine, value]
            out_ref[d] = jnp.concatenate(both, axis=1).astype(out_ref.dtype)


def pack(low, shift, where_at, count, facts, keep, got, cosine, sine):
    out = jax.ShapeDtypeStruct((count, keep.shape[0], 2 * HD), jnp.bfloat16)
    kernel = functools.partial(pack_kernel, low, shift, where_at)
    return small_call(kernel, "pack", (out, out), facts, keep, got, cosine, sine)


def on_device(resid, norm_gain, w_query, w_key, w_value, w_out, cache_key, cache_value, prefix_len):
    blk_count, red_count = lax.axis_size("blk"), lax.axis_size("red")
    blk_at, red_at = lax.axis_index("blk"), lax.axis_index("red")
    start = prefix_len[0]
    mine, width = resid.shape
    far_count = blk_count // 2
    far_at, near_at = blk_at // 2, blk_at % 2
    bits = [1 << k for k in range(red_count.bit_length() - 1)]

    def swap_red(value, bit):
        return lax.ppermute(value, "red", [(k, k ^ bit) for k in range(red_count)])

    def swap_near(value):
        return lax.ppermute(value, "blk", [(k, k ^ 1) for k in range(blk_count)])

    def move_far(value, pairs):
        pairs = [(2 * a + k, 2 * b + k) for a, b in pairs for k in range(2)]
        return lax.ppermute(value, "blk", pairs)

    line = far_count == 4
    if line:
        at_end = (far_at == 0) | (far_at == 3)
        pairs_out = [(1, 0), (2, 3)]
        pairs_in = [(0, 1), (3, 2)]
        middle = [(1, 2), (2, 1)]
        owners = [
            far_at,
            far_at ^ 1,
            far_at ^ jnp.where(at_end, 2, 3),
            far_at ^ jnp.where(at_end, 3, 2),
        ]
    else:
        owners = [(far_at + j) % far_count for j in range(far_count)]

    def spread(own):
        if not line:
            ring = range(far_count)
            return [move_far(own, [((k + j) % far_count, k) for k in ring]) for j in ring if j > 0]
        a1 = move_far(own, pairs_out + pairs_in)
        b1 = move_far(own, middle)
        return [a1, b1, move_far(b1, pairs_out), move_far(a1, middle)]

    def arrive(hops, facts, *others):
        if not line:
            return hops
        a1, b1, a2, b2 = hops
        a3 = move_far(after(b2, *others), pairs_out)
        return [a1, pick(facts, a2, b1), pick(facts, a3, b2)]

    wide = lambda value: value.astype(jnp.float32)

    def add(terms, *others):
        return sum(map(wide, [*terms[:-1], after(terms[-1], *others)])).astype(jnp.float16)

    def collect(parts, passed, first):
        own = [list(terms) for terms in parts[0]]
        if line:
            s2, s3 = parts[2:]
            last = first
            stages = {}

            def go(name, terms, pairs, *others):
                nonlocal last
                last = add(terms, last, *others)
                stages[name] = move_far(last, pairs)

            go("a3", s3[0], pairs_in)
            go("a3+", s3[1], pairs_in)
            go("b2", s3[0] + [stages["a3"]], middle, passed[0])
            go("a2", s2[0], pairs_in)
            go("b2+", s3[1] + [stages["a3+"]], middle, passed[1])
            go("c1", [stages["b2"]], pairs_out)
            go("a2+", s2[1], pairs_in)
            go("b1", s2[0] + [stages["a2"]], middle)
            go("c1+", [stages["b2+"]], pairs_out)
            go("b1+", s2[1] + [stages["a2+"]], middle)
            for k, end in enumerate(("", "+")):
                own[k] += [passed[k], stages["c1" + end], stages["b1" + end]]
        else:
            ring = range(far_count)
            for j in ring:
                for k, terms in enumerate(parts[j] if j > 0 else []):
                    own[k].append(
                        move_far(add(terms), [(i, (i + j) % far_count) for i in ring])
                    )
        return [sum(map(wide, terms)) for terms in own]

    def after(value, *others):
        return lax.optimization_barrier((value, *others))[0] if others else value

    def side_of(bit):
        return (red_at // bit) % 2

    here, few = 2 * mine // red_count, mine // red_count
    low = sum(side_of(bit) * (mine >> k) for k, bit in enumerate(bits) if k > 0)
    bases = [(owner * 2 + (near_at ^ side_of(1))) * mine + low for owner in owners]
    few_low = sum(side_of(bit) * (mine >> (k + 1)) for k, bit in enumerate(bits))
    end = at_end.astype(jnp.int32) if line else jnp.int32(0)
    base_at = 4 + len(bits)
    facts = [start, end, *map(side_of, bits), far_at, near_at, *bases, blk_at * mine + few_low]
    facts = jnp.stack(facts).astype(jnp.int32)

    def sum_rows(keep, got):
        for k, bit in enumerate(bits[1:]):
            keep, send = cut(3 + k, facts, keep, got)
            got = swap_red(send, bit)
        return keep, got

    def join_rows(value, which, *others):
        for k in reversed(which):
            got = after(swap_red(value, bits[k]), *others)
            value = join(2 + k, facts, value, got)
        return value

    head_at = blk_at // (blk_count // KV)
    one_head = lambda value: lax.dynamic_slice_in_dim(value, head_at * HD, HD, 1)
    cached = jnp.concatenate([one_head(cache_key), one_head(cache_value)], axis=1)

    token_at = (facts[base_at:-1, None] + jnp.arange(here, dtype=jnp.int32)).reshape(-1)
    few_at = facts[-1] + jnp.arange(few, dtype=jnp.int32)
    cosine, sine = tables(start + jnp.concatenate([token_at, few_at]))

    total_sq = jnp.sum(resid * resid, axis=1)
    for bit in bits:
        total_sq = total_sq + after(swap_red(total_sq, bit), facts)
    normed = (
        resid * lax.rsqrt(total_sq[:, None] / (width * red_count) + 1e-05) * norm_gain[None, :]
    ).astype(jnp.bfloat16)

    def pieces_of(value):
        return jnp.split(value, PIECES, axis=1)

    slots = range(far_count)
    last = far_count - 1
    hops = spread(normed)
    near = [swap_near(normed)]

    def ask(j, *others):
        return halves(facts, [after(far[j], *others), near[j]], [w_query])

    def have(*hops):
        return hops if line else ()

    def reduce(pair, got, *others):
        return sum_rows(after(pair[0], *others), got)

    def core(pair):
        return swap_red(pair[1], bits[0])

    half = mine // 2
    rest = range(1, len(bits))
    cached = after(cached, normed)[None]
    kv = halves(facts, [normed[:half], normed[half:]], [w_key, w_value])
    kv = reduce(kv, core(kv), near[0], hops[0], *have(hops[1]))
    cached = join_rows(cached, rest, kv[0])
    cached = cached.reshape(red_count // 2, -1, 2 * HD)
    shift = (blk_count // KV).bit_length() - 1
    same, other = pack(
        far_count * here, shift, base_at - 2, far_count, facts, *kv, cosine, sine
    )
    other = swap_near(other)
    far = [normed]
    asked = [ask(0, same, hops[0], *have(hops[1]))]
    moved = [core(asked[0])]
    keys, values = merge(facts, cached, after(swap_red(cached, bits[0]), asked[0][0]))
    far += arrive(hops, facts, asked[0][0])
    near += [swap_near(far[j]) for j in slots[1:]]
    asked.append(ask(1, keys, far[2], *have(hops[-1])))
    moved.append(core(asked[1]))
    fresh = jnp.stack([same, after(other, asked[1][0])], axis=1)
    held, bit = [fresh[d] for d in range(far_count)], 1

    def double(held, bit):
        send = jnp.concatenate(held[1::2])
        got = move_far(send, [(k, k ^ bit) for k in range(far_count)])
        return held[::2], got

    def settle(held, got):
        return [
            jnp.concatenate([one, part])
            for one, part in zip(held, jnp.split(got, len(held)))
        ]

    while len(held) > 2:
        held, got = double(held, bit)
        held = settle(held, got)
        bit *= 2
    held, got = double(held, bit)
    fresh = settle(held, got)[0]
    asked[0] = reduce(asked[0], moved[0], asked[1][0])
    for j in range(2, last):
        asked.append(ask(j, asked[j - 2][0], far[j + 1], fresh))
        moved.append(core(asked[j]))
        if j < last - 1:
            asked[j - 1] = reduce(asked[j - 1], moved[j - 1], asked[j][0])
    rows = here * (w_query.shape[1] // HD)

    def mix(j, new, *others):
        keep, got = asked[j]
        old = [after(keep, *others), got, cosine, sine, keys, values]
        return attend(base_at, far_count, j, facts, here, rows, old, new)

    rest = range(1, len(bits))
    fresh = join_rows(fresh, rest, asked[last - 1][0])
    asked[last - 2] = reduce(asked[last - 2], moved[last - 2], fresh)
    begun = mix(0, None, asked[last - 2][0], fresh)
    fresh = join_rows(fresh, [0], begun[2]).reshape(blk_count * mine, 2 * HD)
    mixed = [None] * far_count
    mixed[0] = attend(base_at, far_count, 0, facts, here, rows, begun, fresh)
    asked.append(ask(last, mixed[0], asked[last - 2][1]))
    moved.append(core(asked[last]))

    parts = [None] * far_count
    per_half = red_count // 2
    turns = [
        sum(bit for i, bit in enumerate(bits[1:]) if k & (per_half >> (i + 1)))
        for k in range(per_half)
    ]
    turns = turns + [turn | bits[0] for turn in turns]

    def share(j):
        return [swap_red(mixed[j], turn) if turn else mixed[j] for turn in turns]

    def project(j, blocks, *others):
        blocks = [after(blocks[0], *others), *blocks[1:]]
        return halves(facts, blocks, [w_out])

    def finish(j, pair, *others):
        keep, send = pair
        send = after(send, *others)
        send = (send * SHRINK).astype(jnp.float16)
        send = [send] if j == 0 else pieces_of(send)
        got = [swap_near(p) for p in send]
        pieces = pieces_of(got[0]) if j == 0 else got
        parts[j] = [[p * SHRINK, g] for p, g in zip(pieces_of(keep), pieces)]
        return send, got

    shared = {0: share(0)}
    asked[last] = reduce(asked[last], moved[last])
    asked[last - 1] = reduce(asked[last - 1], moved[last - 1], asked[last][0])
    mixed[1] = mix(1, fresh, asked[last - 1][0])
    shared[1] = share(1)
    done, got = finish(0, project(0, shared[0], mixed[1], asked[last][1]))
    mixed[last] = mix(last, fresh, *done)
    shared[last] = share(last)
    done, got1 = finish(1, project(1, shared[1], mixed[last]))
    done = [*done, *got]
    for j in range(2, last):
        mixed[j] = mix(j, fresh, *done)
        shared[j] = share(j)
        done = [mixed[j]]
    first = [add(parts[1][0], *done)]
    hop = [(k, k ^ 1) for k in range(far_count)]
    passed = [move_far(first[0], hop)]
    done, _ = finish(last, project(last, shared[last], *done, first[0]))
    first.append(add(parts[1][1], *done, *(p for j in range(2, last) for p in shared[j][1:])))
    passed.append(move_far(first[1], hop))
    done = [*done, first[1]]
    for j in range(2, last):
        done, _ = finish(j, project(j, shared[j], *done))
    return resid + jnp.concatenate(collect(parts, passed, first[1]), axis=1) * (1.0 / SHRINK)


def solution(mesh):
    placed = (
        P("blk", "red"),
        P("red"),
        P("red", "blk"),
        P("red", None),
        P("red", None),
        P("blk", "red"),
        P("red", None),
        P("red", None),
        P(),
    )
    return jax.shard_map(
        on_device, mesh=mesh, in_specs=placed, out_specs=P("blk", "red"), check_vma=False
    )
```
